32 devices in a mesh: seq: 16 (over z, x, core), head: 2 (over y).
Axes of the slice: x: 2, y: 2, z: 4, core: 2. Of those that a mesh axis runs over, the one named last changes fastest.
Arguments:
- queries: float32 [6144, 1024], P('seq', 'head'), may hold values from -1.75 to 1.75
- key_vectors: float32 [6144, 1024], P('seq', 'head'), may hold values from -1.75 to 1.75
- value_vectors: float32 [6144, 1024], P('seq', 'head'), may hold values from -6 to 6
- out_grad: float32 [6144, 1024], P('seq', 'head'), may hold values from -6 to 6
- norm_gain: float32 [1024], P('head'), may hold values from 0.5 to 1.5
- decay_rates: float32 [8], P('head'), may hold values from 1.6276042e-06 to 0.05
- segment_ids: int32 [6144], P('seq'), may hold values from 0 to 5, never falling along the last dimension, each value on 1 to 2048 neighbouring positions
Outputs:
- query_grad: bfloat16 [6144, 1024], P('seq', 'head')
- key_grad: bfloat16 [6144, 1024], P('seq', 'head')
- value_grad: bfloat16 [6144, 1024], P('seq', 'head')
- gain_grad: float32 [1024], P('head')
The draws below stay inside these ranges and needn't reach their ends.
Inputs may be any that keep to these rules, and one draw needn't show every extreme that they name: `segment_ids`: segment numbers never fall along the tokens; each of the 6 segments is one run of 1 to 2048 tokens, and one has exactly 2048.
All inputs are finite; a program needn't handle non-finite values.
Results may differ from the reference program's by a relative error of at most 0.001.
Values sent between devices are 32-bit elements; how exact they have to be, the bound alone decides.
A program may use at most 128 MiB of HBM per device.

```python
import math
import jax
import jax.numpy as jnp
import numpy as np
from jax import lax

HEAD_DIM = 128
TOK_DEV = 384
SEGS = 6
HEADS = 8
FEAT = 1024
TOKENS = 6144
N_SEQ = 16


def level_of(stream_key, extent, split, smallest, top_value):
    factor_of = 1.0
    for position, parts in split:
        heights = jax.random.uniform(jax.random.fold_in(jax.random.fold_in(stream_key, 6), position), (parts,), jnp.float32, smallest / len(split), top_value / len(split))
        factor_of = factor_of * jnp.repeat(jnp.exp(heights), extent[position] // parts).reshape((-1,) + (1,) * (len(extent) - 1 - position))
    return factor_of


def length_profile(amount, total, most, lean):
    loads = [(1 << 20) // math.isqrt(standing ** lean) + 1 for standing in range(2, amount + 1)]
    surplus, counts = total - most - (amount - 1), [1] * (amount - 1)
    while surplus > 0:
        candidates = [i for i in range(amount - 1) if counts[i] < most]
        whole, budget = sum([loads[i] for i in candidates]), surplus
        for i in candidates:
            addition = min(most - counts[i], max(1, budget * loads[i] // whole), surplus)
            counts[i] = counts[i] + addition
            surplus = surplus - addition
    return np.array([most] + counts)


def ragged(rng, amount, total, bound, skew):
    if amount == 2:
        one = jax.random.randint(rng, (), max(1, total - bound), min(bound, total - 1) + 1)
        return jnp.stack([one, total - one])
    lengths = jnp.asarray(length_profile(amount, total, bound, skew), jnp.int32)
    twos = (amount - 1) // 2
    source_of, taker = lengths[1:1 + 2 * twos:2], lengths[2:2 + 2 * twos:2]
    room = jnp.minimum(source_of - 1, bound - taker)
    moved = jax.random.randint(jax.random.fold_in(rng, 1), (twos,), 0, 1 << 20) % (room + 1)
    lengths = lengths.at[1:1 + 2 * twos:2].set(source_of - moved).at[2:2 + 2 * twos:2].set(taker + moved)
    return lengths[jax.random.permutation(jax.random.fold_in(rng, 2), amount)]


def gaussian(key, shape, width, limit, shards=(), held_as=jnp.bfloat16):
    entries = jax.random.normal(key, shape, jnp.float32) * width
    if len(shards) > 0:
        entries = level_of(key, shape, shards, -0.22, 0.18) * entries
    return jnp.clip(entries, min=-limit, max=limit).astype(held_as)


def setup_inputs(seed: int = 0) -> dict:
    key_of = jax.random.split(jax.random.key(seed), 8)
    return {
        "queries": gaussian(key_of[0], (TOKENS, FEAT), 0.3, 1.75, ((0, 16), (1, 2)), jnp.float32),
        "key_vectors": gaussian(key_of[1], (TOKENS, FEAT), 0.3, 1.75, ((0, 16), (1, 2)), jnp.float32),
        "value_vectors": gaussian(key_of[2], (TOKENS, FEAT), 1.0, 6.0, ((0, 16), (1, 2)), jnp.float32),
        "out_grad": gaussian(key_of[3], (TOKENS, FEAT), 1.0, 6.0, ((0, 16), (1, 2)), jnp.float32),
        "norm_gain": jnp.clip(1.0 + 0.1 * jax.random.normal(key_of[4], (FEAT,), jnp.float32), 0.5, 1.5),
        "decay_rates": jnp.clip(jnp.exp(math.log(0.05) - 10.332669 * jax.random.uniform(key_of[5], (HEADS,), jnp.float32) ** level_of(key_of[5], (HEADS,), ((0, 2),), -0.2, 0.2)), 1.6276042060781037e-06, 0.05),
        "segment_ids": jnp.searchsorted(jnp.cumsum(ragged(key_of[6], SEGS, TOKENS, TOKENS // 3, 0)), jnp.arange(TOKENS), side="right").astype(jnp.int32),
    }


PRECISE = lax.Precision.HIGHEST
EPSILON = 1e-06

def block_tables(segs, rates):
    length = segs.shape[0]
    places = jnp.arange(length, dtype=jnp.float32)
    first_seg = segs[0]
    last_seg = segs[length - 1]
    distance = places[:, None] - places[None, :]
    causal = (distance >= 0.0) & (segs[:, None] == segs[None, :])
    weights = jnp.where(causal[None], jnp.exp(-rates[:, None, None] * jnp.maximum(distance, 0.0)[None]), 0.0)
    head_first = (segs == first_seg).astype(jnp.float32)
    tail_last = (segs == last_seg).astype(jnp.float32)
    carry_in_w = jnp.exp(-rates[None, :] * (places[:, None] + 1.0)) * head_first[:, None]
    carry_out_w = jnp.exp(-rates[None, :] * (length - 1.0 - places[:, None])) * tail_last[:, None]
    back_in = jnp.exp(-rates[None, :] * (length - places[:, None])) * tail_last[:, None]
    back_out = jnp.exp(-rates[None, :] * places[:, None]) * head_first[:, None]
    multiplier = jnp.exp(-rates * length) * (first_seg == last_seg).astype(jnp.float32)
    return (weights, carry_in_w, carry_out_w, back_in, back_out, multiplier)

def reference(queries, key_vectors, value_vectors, out_grad, norm_gain, decay_rates, segment_ids):
    head_count = HEADS
    length = TOK_DEV
    features = HEADS * HEAD_DIM
    query_blocks = queries.reshape(N_SEQ, length, head_count, HEAD_DIM)
    key_blocks = key_vectors.reshape(N_SEQ, length, head_count, HEAD_DIM)
    value_blocks = value_vectors.reshape(N_SEQ, length, head_count, HEAD_DIM)
    grad_blocks = out_grad.reshape(N_SEQ, length, features)
    seg_blocks = segment_ids.reshape(N_SEQ, length)
    zero_state = jnp.zeros((head_count, HEAD_DIM, HEAD_DIM), jnp.float32)

    def forward_step(carry, block):
        prev_state, prev_seg = carry
        query_rows, key_rows, value_rows, grad_rows, segs = block
        weights, carry_in_w, carry_out_w, back_in, back_out, multiplier = block_tables(segs, decay_rates)
        first_seg = segs[0].astype(jnp.float32)
        last_seg = segs[length - 1].astype(jnp.float32)
        carry_in = jnp.where(first_seg == prev_seg, 1.0, 0.0).astype(jnp.float32) * prev_state
        scores = jnp.einsum('ihd,jhd->hij', query_rows, key_rows, precision=PRECISE) * weights
        outputs = jnp.einsum('hij,jhd->ihd', scores, value_rows, precision=PRECISE)
        outputs = outputs + carry_in_w[:, :, None] * jnp.einsum('ihd,hde->ihe', query_rows, carry_in, precision=PRECISE)
        flat_out = outputs.reshape(length, features)
        shaped = grad_rows * norm_gain[None, :]
        squares = lax.optimization_barrier(jnp.sum(flat_out * flat_out, axis=1))
        product = lax.optimization_barrier(jnp.sum(shaped * flat_out, axis=1))
        inv_rms = lax.rsqrt(squares / features + EPSILON)
        coef_rms = inv_rms ** 3 * (product / features)
        grad_flat = inv_rms[:, None] * shaped - coef_rms[:, None] * flat_out
        gain_part = lax.optimization_barrier(jnp.sum(grad_rows * flat_out * inv_rms[:, None], axis=0))
        grad_heads = grad_flat.reshape(length, head_count, HEAD_DIM)
        mixed = jnp.einsum('ihe,jhe->hij', grad_heads, value_rows, precision=PRECISE) * weights
        query_grad = jnp.einsum('hij,jhd->ihd', mixed, key_rows, precision=PRECISE)
        query_grad = query_grad + carry_in_w[:, :, None] * jnp.einsum('ihe,hde->ihd', grad_heads, carry_in, precision=PRECISE)
        state_loc = jnp.einsum('jhd,jhe->hde', key_rows * carry_out_w[:, :, None], value_rows, precision=PRECISE)
        new_state = state_loc + multiplier[:, None, None] * carry_in
        return ((new_state, last_seg), (grad_heads, query_grad.astype(jnp.bfloat16), gain_part))
    start_seg = jnp.array(-1.0, dtype=jnp.float32)
    carry_end, results = lax.scan(forward_step, (zero_state, start_seg), (query_blocks, key_blocks, value_blocks, grad_blocks, seg_blocks))
    grad_store, query_grad_blocks, gain_parts = results

    def reverse_step(carry, block):
        next_state, next_seg = carry
        query_rows, key_rows, value_rows, grad_heads, segs = block
        weights, carry_in_w, carry_out_w, back_in, back_out, multiplier = block_tables(segs, decay_rates)
        first_seg = segs[0].astype(jnp.float32)
        last_seg = segs[length - 1].astype(jnp.float32)
        carry_back = jnp.where(last_seg == next_seg, 1.0, 0.0).astype(jnp.float32) * next_state
        scores = jnp.einsum('ihd,jhd->hij', query_rows, key_rows, precision=PRECISE) * weights
        mixed = jnp.einsum('ihe,jhe->hij', grad_heads, value_rows, precision=PRECISE) * weights
        key_grad = jnp.einsum('hij,ihd->jhd', mixed, query_rows, precision=PRECISE)
        key_grad = key_grad + back_in[:, :, None] * jnp.einsum('jhe,hde->jhd', value_rows, carry_back, precision=PRECISE)
        value_grad = jnp.einsum('hij,ihe->jhe', scores, grad_heads, precision=PRECISE)
        value_grad = value_grad + back_in[:, :, None] * jnp.einsum('jhd,hde->jhe', key_rows, carry_back, precision=PRECISE)
        back_loc = jnp.einsum('thd,the->hde', query_rows * back_out[:, :, None], grad_heads, precision=PRECISE)
        new_state = back_loc + multiplier[:, None, None] * carry_back
        return ((new_state, first_seg), (key_grad.astype(jnp.bfloat16), value_grad.astype(jnp.bfloat16)))
    carry_top, back_results = lax.scan(reverse_step, (zero_state, start_seg), (query_blocks, key_blocks, value_blocks, grad_store, seg_blocks), reverse=True)
    key_grad_blocks, value_grad_blocks = back_results
    gain_grad = lax.optimization_barrier(jnp.sum(gain_parts, axis=0))
    return (query_grad_blocks.reshape(N_SEQ * length, features), key_grad_blocks.reshape(N_SEQ * length, features), value_grad_blocks.reshape(N_SEQ * length, features), gain_grad)
```

```python
import functools

import jax
import jax.numpy as jnp
from jax import lax
from jax.experimental import pallas as pl
from jax.experimental.pallas import tpu as pltpu
from jax.sharding import PartitionSpec as P

HEAD_DIM = 128
PAD = HEAD_DIM + 8
EPSILON = 1e-06
F32 = jnp.float32
BF16 = jnp.bfloat16


def split(x):
    hi = x.astype(BF16)
    return hi, (x - hi.astype(F32)).astype(BF16)


def dot(a, b, ca, cb):
    return lax.dot_general(a, b, (((ca,), (cb,)), ((), ())), preferred_element_type=F32)


def cat(parts, axis=1):
    return jnp.concatenate(parts, axis=axis)


def rows_by_rows(a, b):
    return dot(cat([a[0], a[1], a[0]]), cat([b[0], b[0], b[1]]), 1, 1)


def fold(both):
    return both[:, :HEAD_DIM] + both[:, HEAD_DIM:]


def square_by_rows(a, b):
    half = cat([b[0], b[1]])
    return fold(dot(cat(list(a)), cat([half, half], 0), 1, 0))


def square_by_cols(a, b):
    half = cat([b[0], b[1]], 0)
    return fold(dot(cat(list(a)), cat([half, half]), 1, 1))


def tokens_outer(a, b):
    both = fold(dot(cat(list(a)), cat(list(b)), 0, 0))
    return both[:HEAD_DIM] + both[HEAD_DIM:]


def kernel(
    shape, q_hbm, k_hbm, v_hbm, g_hbm, gain_ref, rates, seg_ref,
    qg_ref, kg_ref, vg_ref, gain_out,
    q, k, v, g, w, a_hi, a_lo, p_hi, p_lo, out, grad, cols,
    loc, inbox, gsend, ginbox, csend, carry,
    hsend, hinbox, nsend, ninbox, tsend, tinbox,
    in_sem, st_s, st_r, gr_s, gr_r, ca_s, ca_r, hd_s, hd_r, ng_s, ng_r, nt_s, nt_r,
):
    heads, length, n_seq, n_head, groups, reach = shape
    me = lax.axis_index("seq")
    hx = lax.axis_index("head")
    pos = lax.rem(me, heads)
    z = lax.div(me, heads)
    base = z * heads
    features = float(heads * HEAD_DIM * n_head)

    def load(i, h):
        src, dst = ((k_hbm, k), (v_hbm, v), (q_hbm, q), (g_hbm, g))[i]
        return pltpu.make_async_copy(
            src.at[:, pl.ds(h * HEAD_DIM, HEAD_DIM)], dst.at[h], in_sem.at[i, h]
        )

    for i, h in [(0, h) for h in range(heads)] + [(1, h) for h in range(heads)]:
        load(i, h).start()
    for i in (2, 3):
        for h in range(heads):
            load(i, h).start()

    def remote(src, dst, ss, rs, **where):
        return pltpu.make_async_remote_copy(
            src_ref=src, dst_ref=dst, send_sem=ss, recv_sem=rs,
            device_id=where, device_id_type=pl.DeviceIdType.MESH,
        )

    barrier = pltpu.get_barrier_semaphore()

    def greet(**where):
        pl.semaphore_signal(barrier, inc=1, device_id=where, device_id_type=pl.DeviceIdType.MESH)

    for o in range(1, heads):
        greet(seq=base + lax.rem(pos + o, heads))
    for o in range(1, groups):
        greet(seq=lax.rem(z + o, groups) * heads + pos)
    for o in range(1, n_head):
        greet(head=lax.rem(hx + o, n_head))

    seg_row = seg_ref[...].astype(F32)
    first = seg_row[0:1, 0:1]
    last = seg_row[0:1, length - 1 : length]
    seg_col = jnp.broadcast_to(seg_row, (HEAD_DIM, length)).T
    place = lax.broadcasted_iota(jnp.int32, (length, HEAD_DIM), 0).astype(F32)
    head_first = jnp.where(seg_col == first, 1.0, 0.0)
    tail_last = jnp.where(seg_col == last, 1.0, 0.0)
    for h in range(heads):
        rate = rates[h]
        cols[0, h] = jnp.exp(-rate * (place + 1.0)) * head_first
        cols[1, h] = jnp.exp(-rate * (length - place)) * tail_last

    def send_states(t):
        for h in range(heads):
            @pl.when(h != pos)
            def _(h=h):
                remote(loc.at[t, h], inbox.at[t, pos], st_s.at[t, h], st_r.at[t, pos], seq=base + h).start()

    row_id = lax.broadcasted_iota(jnp.int32, (8, HEAD_DIM), 0)
    meta = jnp.where(row_id == 0, last, jnp.where(row_id == 1, first, 0.0))
    for h in range(heads):
        load(0, h).wait()
        load(1, h).wait()
        out_w = jnp.exp(-rates[h] * (length - 1.0 - place)) * tail_last
        loc[0, h, :HEAD_DIM] = tokens_outer(split(k[h] * out_w), split(v[h]))
        loc[0, h, HEAD_DIM:] = meta
    pl.semaphore_wait(barrier, (heads - 1) + (groups - 1) + (n_head - 1))
    send_states(0)

    def weigh(h):
        rate = rates[h]
        row_w = lax.broadcasted_iota(jnp.int32, (length, length), 0)
        col_w = lax.broadcasted_iota(jnp.int32, (length, length), 1)
        gap = (row_w - col_w).astype(F32)
        same = cat([seg_col] * (length // HEAD_DIM)) == seg_row
        w[h] = jnp.where((gap >= 0.0) & same, jnp.exp(-rate * jnp.maximum(gap, 0.0)), 0.0)

    def score(h):
        hi, lo = split(rows_by_rows(split(q[h]), split(k[h])) * w[h])
        a_hi[h] = hi
        a_lo[h] = lo

    def mix(h):
        hi, lo = split(rows_by_rows(split(grad[h]), split(v[h])) * w[h])
        p_hi[h] = hi
        p_lo[h] = lo

    def by_rows(hi, lo, b):
        return fold(dot(hi, cat(list(b)), 1, 0)) + dot(lo, b[0], 1, 0)

    def by_cols(hi, lo, b):
        return fold(dot(hi, cat(list(b)), 0, 0)) + dot(lo, b[0], 0, 0)

    own_step = jnp.exp(jnp.broadcast_to(-rates[pos] * float(length), (1, HEAD_DIM)))
    own_group = jnp.exp(jnp.broadcast_to(-rates[pos] * float(length * heads), (1, HEAD_DIM)))

    def on_group(t, d, action):
        there = z + d if t == 0 else z - d
        ok = there < groups if t == 0 else there >= 0

        @pl.when(ok)
        def _():
            action(remote(
                gsend.at[t], ginbox.at[t, d - 1], gr_s.at[t, d - 1], gr_r.at[t, d - 1],
                seq=there * heads + pos,
            ))

    def gather_group(t):
        inbox[t, pos] = loc[t, pos]
        for p in range(heads):
            @pl.when(p != pos)
            def _(p=p):
                remote(loc.at[t, p], inbox.at[t, p], st_s.at[t, p], st_r.at[t, p], seq=base + p).wait_recv()
        order = list(range(heads)) if t == 0 else list(range(heads))[::-1]
        near, far = (HEAD_DIM, HEAD_DIM + 1) if t == 0 else (HEAD_DIM + 1, HEAD_DIM)
        total = None
        for i, p in enumerate(order):
            state = inbox[t, p, :HEAD_DIM]
            if i > 0:
                before = order[i - 1]
                keep = inbox[t, before, near : near + 1] == inbox[t, p, far : far + 1]
                came = jnp.where(keep, total, 0.0)
                csend[t, p] = came
                through = inbox[t, p, near : near + 1] == inbox[t, p, far : far + 1]
                total = state + jnp.where(through, own_step, 0.0) * came
            else:
                total = state
        gsend[t, :HEAD_DIM] = total
        gsend[t, HEAD_DIM:] = jnp.broadcast_to(inbox[t, order[-1], near : near + 1], (8, HEAD_DIM))
        for d in range(1, reach + 1):
            on_group(t, d, lambda c: c.start())

    def carry_out(t):
        order = list(range(heads)) if t == 0 else list(range(heads))[::-1]
        near, far = (HEAD_DIM, HEAD_DIM + 1) if t == 0 else (HEAD_DIM + 1, HEAD_DIM)
        for d in range(1, reach + 1):
            there = z - d if t == 0 else z + d
            ok = there >= 0 if t == 0 else there < groups

            @pl.when(ok)
            def _(d=d):
                remote(
                    gsend.at[t], ginbox.at[t, d - 1], gr_s.at[t, d - 1], gr_r.at[t, d - 1], seq=me
                ).wait_recv()

            @pl.when(jnp.logical_not(ok))
            def _(d=d):
                ginbox[t, d - 1] = jnp.full((PAD, HEAD_DIM), -1.0, F32)
        enter = jnp.zeros((HEAD_DIM, HEAD_DIM), F32)
        factor = jnp.ones((1, HEAD_DIM), F32)
        for d in range(1, reach + 1):
            keep = ginbox[t, d - 1, HEAD_DIM : HEAD_DIM + 1] == inbox[t, order[0], far : far + 1]
            enter = enter + jnp.where(keep, factor, 0.0) * ginbox[t, d - 1, :HEAD_DIM]
            factor = factor * own_group
        factor = jnp.ones((1, HEAD_DIM), F32)
        for i, p in enumerate(order):
            if i == 0:
                csend[t, p] = enter
            else:
                before = order[i - 1]
                through = (
                    (inbox[t, before, near : near + 1] == inbox[t, p, far : far + 1])
                    & (inbox[t, before, near : near + 1] == inbox[t, before, far : far + 1])
                )
                factor = factor * jnp.where(through, own_step, 0.0)
                csend[t, p] = csend[t, p] + factor * enter
        for p in range(heads):
            @pl.when(p != pos)
            def _(p=p):
                remote(csend.at[t, p], carry.at[t, pos], ca_s.at[t, p], ca_r.at[t, pos], seq=base + p).start()
        carry[t, pos] = csend[t, pos]

    def wait_carry(t):
        for h in range(heads):
            @pl.when(h != pos)
            def _(h=h):
                remote(csend.at[t, h], carry.at[t, h], ca_s.at[t, h], ca_r.at[t, h], seq=base + h).wait_recv()

    for h in range(heads):
        weigh(h)
    for h in range(heads):
        load(2, h).wait()
    gather_group(0)
    for h in range(heads):
        score(h)
    carry_out(0)
    for h in range(heads):
        out[h] = by_rows(a_hi[h], a_lo[h], split(v[h]))
    for h in range(heads):
        load(3, h).wait()
    wait_carry(0)
    squares = jnp.zeros((length, HEAD_DIM), F32)
    product = jnp.zeros((length, HEAD_DIM), F32)
    for h in range(heads):
        o = out[h] + cols[0, h] * square_by_rows(split(q[h]), split(carry[0, h]))
        out[h] = o
        shaped = g[h] * gain_ref[:, h * HEAD_DIM : (h + 1) * HEAD_DIM]
        grad[h] = shaped
        squares = squares + o * o
        product = product + shaped * o
    sums = cat([
        jnp.sum(squares.T, axis=0, keepdims=True),
        jnp.sum(product.T, axis=0, keepdims=True),
        jnp.zeros((6, length), F32),
    ], 0)
    hsend[...] = sums
    for o in range(1, n_head):
        other = lax.rem(hx + o, n_head)
        remote(hsend, hinbox.at[hx], hd_s.at[o], hd_r.at[hx], head=other).start()
    hinbox[hx] = sums
    for o in range(1, n_head):
        other = lax.rem(hx + o, n_head)
        remote(hsend, hinbox.at[other], hd_s.at[o], hd_r.at[other], head=other).wait_recv()
    sums = hinbox[0]
    for i in range(1, n_head):
        sums = sums + hinbox[i]
    inv_row = lax.rsqrt(sums[0:1] / features + EPSILON)
    coef_row = inv_row * inv_row * inv_row * (sums[1:2] / features)
    inv = jnp.broadcast_to(inv_row, (HEAD_DIM, length)).T
    coef = jnp.broadcast_to(coef_row, (HEAD_DIM, length)).T
    for h in range(heads):
        o = out[h]
        d_out = inv * grad[h] - coef * o
        grad[h] = d_out
        back_w = jnp.exp(-rates[h] * place) * head_first
        loc[1, h, :HEAD_DIM] = tokens_outer(split(q[h] * back_w), split(d_out))
        part = jnp.sum(g[h] * o * inv, axis=0, keepdims=True)
        loc[1, h, HEAD_DIM:] = jnp.where(row_id == 2, part, meta)
    send_states(1)

    for h in range(heads):
        mix(h)
    gather_group(1)
    part = inbox[1, 0, HEAD_DIM:]
    for p in range(1, heads):
        part = part + inbox[1, p, HEAD_DIM:]
    nsend[...] = part
    ninbox[z] = part
    for o in range(1, groups):
        other = lax.rem(z + o, groups)
        remote(nsend, ninbox.at[z], ng_s.at[o], ng_r.at[z], seq=other * heads + pos).start()
    for h in range(heads):
        lanes = pl.ds(h * HEAD_DIM, HEAD_DIM)
        part = by_rows(p_hi[h], p_lo[h], split(k[h]))
        part = part + cols[0, h] * square_by_cols(split(grad[h]), split(carry[0, h]))
        qg_ref[:, lanes] = part.astype(BF16)
    carry_out(1)
    for h in range(heads):
        out[h] = by_cols(p_hi[h], p_lo[h], split(q[h]))
        g[h] = by_cols(a_hi[h], a_lo[h], split(grad[h]))
    for o in range(1, groups):
        other = lax.rem(z + o, groups)
        remote(nsend, ninbox.at[other], ng_s.at[o], ng_r.at[other], seq=me).wait_recv()
    part = ninbox[0]
    for i in range(1, groups):
        part = part + ninbox[i]
    tsend[...] = part
    tinbox[pos] = part
    for p in range(heads):
        @pl.when(p != pos)
        def _(p=p):
            remote(tsend, tinbox.at[pos], nt_s.at[p], nt_r.at[pos], seq=base + p).start()
    wait_carry(1)
    for h in range(heads):
        lanes = pl.ds(h * HEAD_DIM, HEAD_DIM)
        state = split(carry[1, h])
        kg_ref[:, lanes] = (out[h] + cols[1, h] * square_by_cols(split(v[h]), state)).astype(BF16)
        vg_ref[:, lanes] = (g[h] + cols[1, h] * square_by_rows(split(k[h]), state)).astype(BF16)
    for p in range(heads):
        @pl.when(p != pos)
        def _(p=p):
            remote(tsend, tinbox.at[p], nt_s.at[p], nt_r.at[p], seq=base + p).wait_recv()
    for h in range(heads):
        gain_out[:, h * HEAD_DIM : (h + 1) * HEAD_DIM] = tinbox[h, 2:3]

    for t in range(2):
        for h in range(heads):
            @pl.when(h != pos)
            def _(t=t, h=h):
                remote(loc.at[t, h], inbox.at[t, pos], st_s.at[t, h], st_r.at[t, pos], seq=base + h).wait_send()
                remote(csend.at[t, h], carry.at[t, pos], ca_s.at[t, h], ca_r.at[t, pos], seq=base + h).wait_send()
        for d in range(1, reach + 1):
            on_group(t, d, lambda c: c.wait_send())
    for o in range(1, n_head):
        remote(hsend, hinbox.at[hx], hd_s.at[o], hd_r.at[hx], head=lax.rem(hx + o, n_head)).wait_send()
    for o in range(1, groups):
        other = lax.rem(z + o, groups)
        remote(nsend, ninbox.at[z], ng_s.at[o], ng_r.at[z], seq=other * heads + pos).wait_send()
    for p in range(heads):
        @pl.when(p != pos)
        def _(p=p):
            remote(tsend, tinbox.at[pos], nt_s.at[p], nt_r.at[pos], seq=base + p).wait_send()


def body(n_seq, n_head, queries, key_vectors, value_vectors, out_grad, norm_gain, decay_rates, segment_ids):
    length, width = queries.shape
    heads = width // HEAD_DIM
    groups = n_seq // heads
    longest = (length * n_seq) // 3
    blocks = -(-(longest - 1) // length)
    reach = min(-(-blocks // heads), groups - 1)
    shape = (heads, length, n_seq, n_head, groups, reach)
    any_spec = pl.BlockSpec(memory_space=pl.ANY)
    vmem = pl.BlockSpec(memory_space=pltpu.VMEM)
    tok = (heads, length, HEAD_DIM)
    sq = (heads, length, length)
    dma = pltpu.SemaphoreType.DMA
    outs = pl.pallas_call(
        functools.partial(kernel, shape),
        out_shape=(
            jax.ShapeDtypeStruct((length, width), BF16),
            jax.ShapeDtypeStruct((length, width), BF16),
            jax.ShapeDtypeStruct((length, width), BF16),
            jax.ShapeDtypeStruct((1, width), F32),
        ),
        in_specs=[any_spec] * 4 + [vmem, pl.BlockSpec(memory_space=pltpu.SMEM), vmem],
        out_specs=(vmem,) * 4,
        scratch_shapes=[
            pltpu.VMEM(tok, F32), pltpu.VMEM(tok, F32), pltpu.VMEM(tok, F32), pltpu.VMEM(tok, F32),
            pltpu.VMEM(sq, F32),
            pltpu.VMEM(sq, BF16), pltpu.VMEM(sq, BF16), pltpu.VMEM(sq, BF16), pltpu.VMEM(sq, BF16),
            pltpu.VMEM(tok, F32), pltpu.VMEM(tok, F32),
            pltpu.VMEM((2,) + tok, F32),
            pltpu.VMEM((2, heads, PAD, HEAD_DIM), F32),
            pltpu.VMEM((2, heads, PAD, HEAD_DIM), F32),
            pltpu.VMEM((2, PAD, HEAD_DIM), F32),
            pltpu.VMEM((2, reach, PAD, HEAD_DIM), F32),
            pltpu.VMEM((2, heads, HEAD_DIM, HEAD_DIM), F32),
            pltpu.VMEM((2, heads, HEAD_DIM, HEAD_DIM), F32),
            pltpu.VMEM((8, length), F32),
            pltpu.VMEM((n_head, 8, length), F32),
            pltpu.VMEM((8, HEAD_DIM), F32),
            pltpu.VMEM((groups, 8, HEAD_DIM), F32),
            pltpu.VMEM((8, HEAD_DIM), F32),
            pltpu.VMEM((heads, 8, HEAD_DIM), F32),
            dma((4, heads)),
            dma((2, heads)), dma((2, heads)),
            dma((2, reach)), dma((2, reach)),
            dma((2, heads)), dma((2, heads)),
            dma((n_head,)), dma((n_head,)),
            dma((groups,)), dma((groups,)),
            dma((heads,)), dma((heads,)),
        ],
        compiler_params=pltpu.CompilerParams(
            collective_id=0, has_side_effects=True, vmem_limit_bytes=40 * 1024 * 1024
        ),
        name="decayed_attention_grad",
    )(
        queries, key_vectors, value_vectors, out_grad,
        norm_gain.reshape(1, width), decay_rates, segment_ids.reshape(1, length),
    )
    return outs[0], outs[1], outs[2], outs[3].reshape(width)


def solution(mesh):
    return jax.shard_map(
        functools.partial(body, mesh.shape["seq"], mesh.shape["head"]),
        mesh=mesh,
        in_specs=(
            P("seq", "head"),
            P("seq", "head"),
            P("seq", "head"),
            P("seq", "head"),
            P("head"),
            P("head"),
            P("seq"),
        ),
        out_specs=(P("seq", "head"), P("seq", "head"), P("seq", "head"), P("head")),
        check_vma=False,
    )
```

```python
import functools

import jax
import jax.numpy as jnp
from jax import lax
from jax.experimental import pallas as pl
from jax.experimental.pallas import tpu as pltpu
from jax.sharding import PartitionSpec as P

HEAD_DIM = 128
CHUNKS = 2
ROWS = HEAD_DIM // CHUNKS
PAD = ROWS + 8
CORES = 2
VMEM_BYTES = 63 * 1024 * 1024
EPSILON = 1e-06
F32 = jnp.float32
BF16 = jnp.bfloat16


def split(x):
    hi = x.astype(BF16)
    return hi, (x - hi.astype(F32)).astype(BF16)


def dot(a, b, ca, cb):
    return lax.dot_general(a, b, (((ca,), (cb,)), ((), ())), preferred_element_type=F32)


def cat(parts, axis=1):
    return jnp.concatenate(parts, axis=axis)


def rows_by_rows(a, b):
    return dot(cat([a[0], a[1], a[0]]), cat([b[0], b[0], b[1]]), 1, 1)


def fold(both):
    return both[:, :HEAD_DIM] + both[:, HEAD_DIM:]


def square_by_rows(a, b):
    half = cat([b[0], b[1]])
    return fold(dot(cat(list(a)), cat([half, half], 0), 1, 0))


def square_by_cols(a, b):
    half = cat([b[0], b[1]], 0)
    return fold(dot(cat(list(a)), cat([half, half]), 1, 1))


def turned(x):
    return cat(list(split(x.T)), 0)


def outer(a_t, b):
    both = fold(dot(a_t, cat(list(split(b))), 1, 0))
    return both[:HEAD_DIM] + both[HEAD_DIM:]


def under(a_t, hi, lo):
    both = dot(a_t, hi, 1, 0)
    return (both[:HEAD_DIM] + both[HEAD_DIM:] + dot(a_t[:HEAD_DIM], lo, 1, 0)).T


def kernel(
    shape, q_hbm, k_hbm, v_hbm, g_hbm, gain_ref, rates, seg_ref,
    qg_ref, kg_ref, vg_ref, gain_out,
    q, k, v, g, w, a_hi, a_lo, p_hi, p_lo, out, grad, cols, q_t,
    loc, inbox, gsend, ginbox, csend, carry,
    hsend, hinbox, nsend, ninbox, tsend, tinbox,
    in_sem, st_s, st_r, gr_s, gr_r, ca_s, ca_r, hd_s, hd_r, ng_s, ng_r, nt_s, nt_r,
):
    heads, length, n_seq, n_head, groups, reach = shape
    me = lax.axis_index("seq")
    hx = lax.axis_index("head")
    pos = lax.rem(me, heads)
    z = lax.div(me, heads)
    base = z * heads
    features = float(heads * HEAD_DIM * n_head)

    def load(i, h):
        src, dst = ((k_hbm, k), (v_hbm, v), (q_hbm, q), (g_hbm, g))[i]
        return pltpu.make_async_copy(
            src.at[:, pl.ds(h * HEAD_DIM, HEAD_DIM)], dst.at[h], in_sem.at[i, h]
        )

    for i, h in [(0, h) for h in range(heads)] + [(1, h) for h in range(heads)]:
        load(i, h).start()
    for i in (2, 3):
        for h in range(heads):
            load(i, h).start()

    def remote(src, dst, ss, rs, **where):
        return pltpu.make_async_remote_copy(
            src_ref=src, dst_ref=dst, send_sem=ss, recv_sem=rs,
            device_id=where, device_id_type=pl.DeviceIdType.MESH,
        )

    barrier = pltpu.get_barrier_semaphore()

    def greet(**where):
        pl.semaphore_signal(barrier, inc=1, device_id=where, device_id_type=pl.DeviceIdType.MESH)

    for o in range(1, heads):
        greet(seq=base + lax.rem(pos + o, heads))
    for o in range(1, groups):
        greet(seq=lax.rem(z + o, groups) * heads + pos)
    for o in range(1, n_head):
        greet(head=lax.rem(hx + o, n_head))

    seg_row = seg_ref[...].reshape(1, length).astype(F32)
    first = seg_row[0:1, 0:1]
    last = seg_row[0:1, length - 1 : length]
    seg_col = jnp.broadcast_to(seg_row, (HEAD_DIM, length)).T
    place = lax.broadcasted_iota(jnp.int32, (length, HEAD_DIM), 0).astype(F32)
    head_first = jnp.where(seg_col == first, 1.0, 0.0)
    tail_last = jnp.where(seg_col == last, 1.0, 0.0)
    for h in range(heads):
        rate = rates[h]
        cols[0, h] = jnp.exp(-rate * (place + 1.0)) * head_first
        cols[1, h] = jnp.exp(-rate * (length - place)) * tail_last

    side = lax.div(pos, CORES)
    sides = heads // CORES

    def post(t, members):
        for c in range(CHUNKS):
            for m in members:
                remote(
                    loc.at[t, m, c], inbox.at[t, pos, c], st_s.at[t, m, c], st_r.at[t, pos, c], seq=base + m
                ).start()

    def put(t, m, state, tail):
        for c in range(CHUNKS):
            loc[t, m, c, :ROWS] = state[c * ROWS : (c + 1) * ROWS]
            loc[t, m, c, ROWS:] = tail

    def others(o):
        there = lax.rem(side + o, sides) * CORES
        return [there + i for i in range(CORES)]

    mates = [side * CORES + lax.rem(pos - side * CORES + i, CORES) for i in range(1, CORES)]
    rounds = [others(o) for o in range(1, sides)] + [mates]

    row_id = lax.broadcasted_iota(jnp.int32, (8, HEAD_DIM), 0)
    meta = jnp.where(row_id == 0, last, jnp.where(row_id == 1, first, 0.0))

    def local_state(m):
        out_w = jnp.exp(-rates[m] * (length - 1.0 - place)) * tail_last
        put(0, m, outer(turned(k[m]), v[m] * out_w), meta)

    for h in range(heads):
        load(0, h).wait()
        load(1, h).wait()
    for i, members in enumerate(rounds):
        for m in members:
            local_state(m)
        if i == 0:
            pl.semaphore_wait(barrier, (heads - 1) + (groups - 1) + (n_head - 1))
        post(0, members)
    local_state(pos)

    def weigh(h):
        rate = rates[h]
        row_w = lax.broadcasted_iota(jnp.int32, (length, length), 0)
        col_w = lax.broadcasted_iota(jnp.int32, (length, length), 1)
        gap = (row_w - col_w).astype(F32)
        same = cat([seg_col] * (length // HEAD_DIM)) == seg_row
        w[h] = jnp.where((gap >= 0.0) & same, jnp.exp(-rate * jnp.maximum(gap, 0.0)), 0.0)

    def score(h):
        hi, lo = split(rows_by_rows(split(q[h]), split(k[h])) * w[h])
        a_hi[h] = hi
        a_lo[h] = lo

    def mix(h):
        hi, lo = split(rows_by_rows(split(grad[h]), split(v[h])) * w[h])
        p_hi[h] = hi
        p_lo[h] = lo

    def by_rows(hi, lo, b):
        return fold(dot(hi, cat(list(b)), 1, 0)) + dot(lo, b[0], 1, 0)

    own_step = jnp.exp(jnp.broadcast_to(-rates[pos] * float(length), (1, HEAD_DIM)))
    own_group = jnp.exp(jnp.broadcast_to(-rates[pos] * float(length * heads), (1, HEAD_DIM)))

    def on_group(t, d, c, action):
        there = z + d if t == 0 else z - d
        ok = there < groups if t == 0 else there >= 0

        @pl.when(ok)
        def _():
            action(remote(
                gsend.at[t, c], ginbox.at[t, d - 1, c], gr_s.at[t, d - 1, c], gr_r.at[t, d - 1, c],
                seq=there * heads + pos,
            ))

    def direction(t):
        order = list(range(heads))
        return (order, ROWS, ROWS + 1) if t == 0 else (order[::-1], ROWS + 1, ROWS)

    def gather_group(t, c):
        inbox[t, pos, c] = loc[t, pos, c]
        for p in range(heads):
            @pl.when(p != pos)
            def _(p=p):
                remote(
                    loc.at[t, p, c], inbox.at[t, p, c], st_s.at[t, p, c], st_r.at[t, p, c], seq=base + p
                ).wait_recv()
        order, near, far = direction(t)
        total = None
        for i, p in enumerate(order):
            state = inbox[t, p, c, :ROWS]
            if i > 0:
                before = order[i - 1]
                keep = inbox[t, before, c, near : near + 1] == inbox[t, p, c, far : far + 1]
                came = jnp.where(keep, total, 0.0)
                csend[t, p, c] = came
                through = inbox[t, p, c, near : near + 1] == inbox[t, p, c, far : far + 1]
                total = state + jnp.where(through, own_step, 0.0) * came
            else:
                total = state
        gsend[t, c, :ROWS] = total
        gsend[t, c, ROWS:] = jnp.broadcast_to(inbox[t, order[-1], c, near : near + 1], (8, HEAD_DIM))
        for d in range(1, reach + 1):
            on_group(t, d, c, lambda copy: copy.start())

    def carry_out(t, c):
        order, near, far = direction(t)
        for d in range(1, reach + 1):
            there = z - d if t == 0 else z + d
            ok = there >= 0 if t == 0 else there < groups

            @pl.when(ok)
            def _(d=d):
                remote(
                    gsend.at[t, c], ginbox.at[t, d - 1, c], gr_s.at[t, d - 1, c], gr_r.at[t, d - 1, c],
                    seq=lax.rem(me + heads, n_seq),
                ).wait_recv()

            @pl.when(jnp.logical_not(ok))
            def _(d=d):
                ginbox[t, d - 1, c] = jnp.full((PAD, HEAD_DIM), -1.0, F32)
        enter = jnp.zeros((ROWS, HEAD_DIM), F32)
        factor = jnp.ones((1, HEAD_DIM), F32)
        for d in range(1, reach + 1):
            keep = ginbox[t, d - 1, c, ROWS : ROWS + 1] == inbox[t, order[0], c, far : far + 1]
            enter = enter + jnp.where(keep, factor, 0.0) * ginbox[t, d - 1, c, :ROWS]
            factor = factor * own_group
        factor = jnp.ones((1, HEAD_DIM), F32)
        for i, p in enumerate(order):
            if i == 0:
                csend[t, p, c] = enter
            else:
                before = order[i - 1]
                through = (
                    (inbox[t, before, c, near : near + 1] == inbox[t, p, c, far : far + 1])
                    & (inbox[t, before, c, near : near + 1] == inbox[t, before, c, far : far + 1])
                )
                factor = factor * jnp.where(through, own_step, 0.0)
                csend[t, p, c] = csend[t, p, c] + factor * enter
        for m in [m for members in rounds for m in members]:
            remote(
                csend.at[t, m, c], carry.at[t, pos, c], ca_s.at[t, m, c], ca_r.at[t, pos, c], seq=base + m
            ).start()
        carry[t, pos, c] = csend[t, pos, c]

    def wait_carry(t):
        for c in range(CHUNKS):
            for m in [m for members in rounds for m in members]:
                remote(
                    csend.at[t, m, c], carry.at[t, m, c], ca_s.at[t, m, c], ca_r.at[t, m, c], seq=base + m
                ).wait_recv()

    def carried(t, h):
        return split(carry[t, h].reshape(HEAD_DIM, HEAD_DIM))

    def weave(work, steps, lead):
        rest = max(len(work) - lead, 1)
        done = 0
        for i, piece in enumerate(work):
            piece()
            due = (i + 1 - lead) * len(steps) // rest if i + 1 > lead else 0
            while done < min(due, len(steps)):
                steps[done]()
                done += 1
        while done < len(steps):
            steps[done]()
            done += 1

    def turn(h):
        q_t[h] = turned(q[h])

    def intra(h):
        out[h] = by_rows(a_hi[h], a_lo[h], split(v[h]))

    def each(f):
        return [functools.partial(f, h) for h in range(heads)]

    def chunks(f, t):
        return [functools.partial(f, t, c) for c in range(CHUNKS)]

    for h in range(heads):
        weigh(h)
    for h in range(heads):
        load(2, h).wait()
    weave(each(score) + each(turn) + each(intra), chunks(gather_group, 0) + chunks(carry_out, 0), 1)
    for h in range(heads):
        load(3, h).wait()
    wait_carry(0)
    squares = jnp.zeros((length, HEAD_DIM), F32)
    product = jnp.zeros((length, HEAD_DIM), F32)
    for h in range(heads):
        o = out[h] + cols[0, h] * square_by_rows(split(q[h]), carried(0, h))
        out[h] = o
        shaped = g[h] * gain_ref[:, h * HEAD_DIM : (h + 1) * HEAD_DIM]
        grad[h] = shaped
        squares = squares + o * o
        product = product + shaped * o
    sums = cat([
        jnp.sum(squares.T, axis=0, keepdims=True),
        jnp.sum(product.T, axis=0, keepdims=True),
        jnp.zeros((6, length), F32),
    ], 0)
    hsend[...] = sums
    for o in range(1, n_head):
        other = lax.rem(hx + o, n_head)
        remote(hsend, hinbox.at[hx], hd_s.at[o], hd_r.at[hx], head=other).start()
    hinbox[hx] = sums
    for o in range(1, n_head):
        other = lax.rem(hx + o, n_head)
        remote(hsend, hinbox.at[other], hd_s.at[o], hd_r.at[other], head=other).wait_recv()
    sums = hinbox[0]
    for i in range(1, n_head):
        sums = sums + hinbox[i]
    inv_row = lax.rsqrt(sums[0:1] / features + EPSILON)
    coef_row = inv_row * inv_row * inv_row * (sums[1:2] / features)
    inv = jnp.broadcast_to(inv_row, (HEAD_DIM, length)).T
    coef = jnp.broadcast_to(coef_row, (HEAD_DIM, length)).T

    def local_back(m):
        o = out[m]
        d_out = inv * grad[m] - coef * o
        grad[m] = d_out
        back_w = jnp.exp(-rates[m] * place) * head_first
        part = jnp.sum(g[m] * o * inv, axis=0, keepdims=True)
        put(1, m, outer(q_t[m], d_out * back_w), jnp.where(row_id == 2, part, meta))

    for members in rounds:
        for m in members:
            local_back(m)
        post(1, members)
    local_back(pos)

    def group_gain():
        part = inbox[1, 0, 0, ROWS:]
        for p in range(1, heads):
            part = part + inbox[1, p, 0, ROWS:]
        nsend[...] = part
        ninbox[z] = part
        for o in range(1, groups):
            other = lax.rem(z + o, groups)
            remote(nsend, ninbox.at[z], ng_s.at[o], ng_r.at[z], seq=other * heads + pos).start()

    def whole_gain():
        for o in range(1, groups):
            other = lax.rem(z + o, groups)
            remote(nsend, ninbox.at[other], ng_s.at[o], ng_r.at[other], seq=other * heads + pos).wait_recv()
        part = ninbox[0]
        for i in range(1, groups):
            part = part + ninbox[i]
        tsend[...] = part
        tinbox[pos] = part
        for p in range(heads):
            @pl.when(p != pos)
            def _(p=p):
                remote(tsend, tinbox.at[pos], nt_s.at[p], nt_r.at[pos], seq=base + p).start()

    def for_queries(h):
        lanes = pl.ds(h * HEAD_DIM, HEAD_DIM)
        part = by_rows(p_hi[h], p_lo[h], split(k[h]))
        part = part + cols[0, h] * square_by_cols(split(grad[h]), carried(0, h))
        qg_ref[:, lanes] = part.astype(BF16)

    def for_keys(h):
        out[h] = under(q_t[h], p_hi[h], p_lo[h])

    def for_values(h):
        g[h] = under(turned(grad[h]), a_hi[h], a_lo[h])

    steps = chunks(gather_group, 1) + [group_gain] + chunks(carry_out, 1) + [whole_gain]
    weave(each(mix) + each(for_queries) + each(for_keys) + each(for_values), steps, heads)
    wait_carry(1)
    for h in range(heads):
        lanes = pl.ds(h * HEAD_DIM, HEAD_DIM)
        state = carried(1, h)
        kg_ref[:, lanes] = (out[h] + cols[1, h] * square_by_cols(split(v[h]), state)).astype(BF16)
        vg_ref[:, lanes] = (g[h] + cols[1, h] * square_by_rows(split(k[h]), state)).astype(BF16)
    for p in range(heads):
        @pl.when(p != pos)
        def _(p=p):
            remote(tsend, tinbox.at[p], nt_s.at[p], nt_r.at[p], seq=base + p).wait_recv()
    for h in range(heads):
        gain_out[:, h * HEAD_DIM : (h + 1) * HEAD_DIM] = tinbox[h, 2:3]

    for t in range(2):
        for c in range(CHUNKS):
            for m in [m for members in rounds for m in members]:
                remote(
                    loc.at[t, m, c], inbox.at[t, pos, c], st_s.at[t, m, c], st_r.at[t, pos, c], seq=base + m
                ).wait_send()
                remote(
                    csend.at[t, m, c], carry.at[t, pos, c], ca_s.at[t, m, c], ca_r.at[t, pos, c], seq=base + m
                ).wait_send()
            for d in range(1, reach + 1):
                on_group(t, d, c, lambda copy: copy.wait_send())
    for o in range(1, n_head):
        remote(hsend, hinbox.at[hx], hd_s.at[o], hd_r.at[hx], head=lax.rem(hx + o, n_head)).wait_send()
    for o in range(1, groups):
        other = lax.rem(z + o, groups)
        remote(nsend, ninbox.at[z], ng_s.at[o], ng_r.at[z], seq=other * heads + pos).wait_send()
    for p in range(heads):
        @pl.when(p != pos)
        def _(p=p):
            remote(tsend, tinbox.at[pos], nt_s.at[p], nt_r.at[pos], seq=base + p).wait_send()


def store(*refs):
    sem = refs[-1]
    copies = [pltpu.make_async_copy(refs[i], refs[4 + i], sem.at[i]) for i in range(4)]
    for copy in copies:
        copy.start()
    for copy in copies:
        copy.wait()


def body(n_seq, n_head, queries, key_vectors, value_vectors, out_grad, norm_gain, decay_rates, segment_ids):
    length, width = queries.shape
    heads = width // HEAD_DIM
    groups = n_seq // heads
    longest = (length * n_seq) // 3
    blocks = -(-(longest - 1) // length)
    reach = min(-(-blocks // heads), groups - 1)
    shape = (heads, length, n_seq, n_head, groups, reach)
    any_spec = pl.BlockSpec(memory_space=pl.ANY)
    vmem = pl.BlockSpec(memory_space=pltpu.VMEM)
    tok = (heads, length, HEAD_DIM)
    sq = (heads, length, length)
    dma = pltpu.SemaphoreType.DMA
    outs = pl.pallas_call(
        functools.partial(kernel, shape),
        out_shape=(
            jax.ShapeDtypeStruct((length, width), BF16),
            jax.ShapeDtypeStruct((length, width), BF16),
            jax.ShapeDtypeStruct((length, width), BF16),
            jax.ShapeDtypeStruct((1, width), F32),
        ),
        in_specs=[any_spec] * 4 + [vmem, pl.BlockSpec(memory_space=pltpu.SMEM), vmem],
        out_specs=(vmem,) * 4,
        scratch_shapes=[
            pltpu.VMEM(tok, F32), pltpu.VMEM(tok, F32), pltpu.VMEM(tok, F32), pltpu.VMEM(tok, F32),
            pltpu.VMEM(sq, F32),
            pltpu.VMEM(sq, BF16), pltpu.VMEM(sq, BF16), pltpu.VMEM(sq, BF16), pltpu.VMEM(sq, BF16),
            pltpu.VMEM(tok, F32), pltpu.VMEM(tok, F32),
            pltpu.VMEM((2,) + tok, F32),
            pltpu.VMEM((heads, 2 * HEAD_DIM, length), BF16),
            pltpu.VMEM((2, heads, CHUNKS, PAD, HEAD_DIM), F32),
            pltpu.VMEM((2, heads, CHUNKS, PAD, HEAD_DIM), F32),
            pltpu.VMEM((2, CHUNKS, PAD, HEAD_DIM), F32),
            pltpu.VMEM((2, reach, CHUNKS, PAD, HEAD_DIM), F32),
            pltpu.VMEM((2, heads, CHUNKS, ROWS, HEAD_DIM), F32),
            pltpu.VMEM((2, heads, CHUNKS, ROWS, HEAD_DIM), F32),
            pltpu.VMEM((8, length), F32),
            pltpu.VMEM((n_head, 8, length), F32),
            pltpu.VMEM((8, HEAD_DIM), F32),
            pltpu.VMEM((groups, 8, HEAD_DIM), F32),
            pltpu.VMEM((8, HEAD_DIM), F32),
            pltpu.VMEM((heads, 8, HEAD_DIM), F32),
            dma((4, heads)),
            dma((2, heads, CHUNKS)), dma((2, heads, CHUNKS)),
            dma((2, reach, CHUNKS)), dma((2, reach, CHUNKS)),
            dma((2, heads, CHUNKS)), dma((2, heads, CHUNKS)),
            dma((n_head,)), dma((n_head,)),
            dma((groups,)), dma((groups,)),
            dma((heads,)), dma((heads,)),
        ],
        compiler_params=pltpu.CompilerParams(
            collective_id=0, has_side_effects=True, vmem_limit_bytes=VMEM_BYTES
        ),
        name="decayed_attention_grad",
    )(
        queries, key_vectors, value_vectors, out_grad,
        norm_gain.reshape(1, width), decay_rates, segment_ids,
    )
    outs = pl.pallas_call(
        store,
        out_shape=tuple(jax.ShapeDtypeStruct(x.shape, x.dtype) for x in outs),
        in_specs=[any_spec] * 4,
        out_specs=(any_spec,) * 4,
        scratch_shapes=[dma((4,))],
        compiler_params=pltpu.CompilerParams(vmem_limit_bytes=VMEM_BYTES),
        name="store_results",
    )(*outs)
    return outs[0], outs[1], outs[2], outs[3].reshape(width)


def solution(mesh):
    return jax.shard_map(
        functools.partial(body, mesh.shape["seq"], mesh.shape["head"]),
        mesh=mesh,
        in_specs=(
            P("seq", "head"),
            P("seq", "head"),
            P("seq", "head"),
            P("seq", "head"),
            P("head"),
            P("head"),
            P("seq"),
        ),
        out_specs=(P("seq", "head"), P("seq", "head"), P("seq", "head"), P("head")),
        check_vma=False,
    )
```

```python
import functools

import jax
import jax.numpy as jnp
from jax import lax
from jax.experimental import pallas as pl
from jax.experimental.pallas import tpu as pltpu
from jax.sharding import PartitionSpec as P

HEAD_DIM = 128
CHUNKS = 2
ROWS = HEAD_DIM // CHUNKS
PAD = ROWS + 8
CORES = 2
VMEM_BYTES = 63 * 1024 * 1024
EPSILON = 1e-06
F32 = jnp.float32
BF16 = jnp.bfloat16


def split(x):
    hi = x.astype(BF16)
    return hi, (x - hi.astype(F32)).astype(BF16)


def dot(a, b, ca, cb):
    return lax.dot_general(a, b, (((ca,), (cb,)), ((), ())), preferred_element_type=F32)


def cat(parts, axis=1):
    return jnp.concatenate(parts, axis=axis)


def rows_by_rows(a, b):
    return dot(cat([a[0], a[1], a[0]]), cat([b[0], b[0], b[1]]), 1, 1)


def fold(both):
    return both[:, :HEAD_DIM] + both[:, HEAD_DIM:]


def square_by_rows(a, b):
    half = cat([b[0], b[1]])
    return fold(dot(cat(list(a)), cat([half, half], 0), 1, 0))


def square_by_cols(a, b):
    half = cat([b[0], b[1]], 0)
    return fold(dot(cat(list(a)), cat([half, half]), 1, 1))


def turned(x):
    return cat(list(split(x.T)), 0)


def outer(a_t, b):
    both = fold(dot(a_t, cat(list(split(b))), 1, 0))
    return both[:HEAD_DIM] + both[HEAD_DIM:]


def under(a_t, hi, lo):
    both = dot(a_t, hi, 1, 0)
    return (both[:HEAD_DIM] + both[HEAD_DIM:] + dot(a_t[:HEAD_DIM], lo, 1, 0)).T


def kernel(
    shape, q_hbm, k_hbm, v_hbm, g_hbm, gain_ref, rates, seg_ref,
    qg_ref, kg_ref, vg_ref, gain_out,
    q, k, v, g, w, a_hi, a_lo, p_hi, p_lo, out, grad, cols, q_t,
    loc, inbox, gsend, ginbox, csend, carry,
    hsend, hinbox, nsend, ninbox, tsend, tinbox,
    in_sem, st_s, st_r, gr_s, gr_r, ca_s, ca_r, hd_s, hd_r, ng_s, ng_r, nt_s, nt_r,
):
    heads, length, n_seq, n_head, groups, reach = shape
    me = lax.axis_index("seq")
    hx = lax.axis_index("head")
    pos = lax.rem(me, heads)
    z = lax.div(me, heads)
    base = z * heads
    features = float(heads * HEAD_DIM * n_head)

    def lanes_of(h):
        return pl.ds(pl.multiple_of(h * HEAD_DIM, HEAD_DIM), HEAD_DIM)

    def load(i, h):
        src, dst = ((k_hbm, k), (v_hbm, v), (q_hbm, q), (g_hbm, g))[i]
        return pltpu.make_async_copy(
            src.at[:, lanes_of(h)], dst.at[h], in_sem.at[i, h]
        )

    side = lax.div(pos, CORES)
    sides = heads // CORES

    def others(o):
        there = lax.rem(side + o, sides) * CORES
        return [there + i for i in range(CORES)]

    mates = [side * CORES + lax.rem(pos - side * CORES + i, CORES) for i in range(1, CORES)]
    rounds = [others(o) for o in range(1, sides)] + [mates]
    peers = [m for members in rounds for m in members]

    for m in peers + [pos]:
        load(0, m).start()
        load(1, m).start()
    for i in (2, 3):
        for m in range(heads):
            load(i, m).start()

    def remote(src, dst, ss, rs, **where):
        return pltpu.make_async_remote_copy(
            src_ref=src, dst_ref=dst, send_sem=ss, recv_sem=rs,
            device_id=where, device_id_type=pl.DeviceIdType.MESH,
        )

    barrier = pltpu.get_barrier_semaphore()

    def greet(**where):
        pl.semaphore_signal(barrier, inc=1, device_id=where, device_id_type=pl.DeviceIdType.MESH)

    for o in range(1, heads):
        greet(seq=base + lax.rem(pos + o, heads))
    for o in range(1, groups):
        greet(seq=lax.rem(z + o, groups) * heads + pos)
    for o in range(1, n_head):
        greet(head=lax.rem(hx + o, n_head))

    seg_row = seg_ref[...].reshape(1, length).astype(F32)
    first = seg_row[0:1, 0:1]
    last = seg_row[0:1, length - 1 : length]
    seg_col = jnp.broadcast_to(seg_row, (HEAD_DIM, length)).T
    place = lax.broadcasted_iota(jnp.int32, (length, HEAD_DIM), 0).astype(F32)
    head_first = jnp.where(seg_col == first, 1.0, 0.0)
    tail_last = jnp.where(seg_col == last, 1.0, 0.0)
    for h in range(heads):
        rate = rates[h]
        cols[0, h] = jnp.exp(-rate * (place + 1.0)) * head_first
        cols[1, h] = jnp.exp(-rate * (length - place)) * tail_last

    def post(t, members):
        for c in range(CHUNKS):
            for m in members:
                remote(
                    loc.at[t, m, c], inbox.at[t, pos, c], st_s.at[t, m, c], st_r.at[t, pos, c], seq=base + m
                ).start()

    def put(t, m, state, tail):
        for c in range(CHUNKS):
            loc[t, m, c, :ROWS] = state[c * ROWS : (c + 1) * ROWS]
            loc[t, m, c, ROWS:] = tail

    row_id = lax.broadcasted_iota(jnp.int32, (8, HEAD_DIM), 0)
    meta = jnp.where(row_id == 0, last, jnp.where(row_id == 1, first, 0.0))

    def local_state(m):
        load(0, m).wait()
        load(1, m).wait()
        out_w = jnp.exp(-rates[m] * (length - 1.0 - place)) * tail_last
        put(0, m, outer(turned(k[m]), v[m] * out_w), meta)

    for i, members in enumerate(rounds):
        for m in members:
            local_state(m)
        if i == 0:
            pl.semaphore_wait(barrier, (heads - 1) + (groups - 1) + (n_head - 1))
        post(0, members)
    local_state(pos)

    def weigh(h):
        rate = rates[h]
        row_w = lax.broadcasted_iota(jnp.int32, (length, length), 0)
        col_w = lax.broadcasted_iota(jnp.int32, (length, length), 1)
        gap = (row_w - col_w).astype(F32)
        same = cat([seg_col] * (length // HEAD_DIM)) == seg_row
        w[h] = jnp.where((gap >= 0.0) & same, jnp.exp(-rate * jnp.maximum(gap, 0.0)), 0.0)

    def score(h):
        hi, lo = split(rows_by_rows(split(q[h]), split(k[h])) * w[h])
        a_hi[h] = hi
        a_lo[h] = lo

    def mix(h):
        hi, lo = split(rows_by_rows(split(grad[h]), split(v[h])) * w[h])
        p_hi[h] = hi
        p_lo[h] = lo

    def by_rows(hi, lo, b):
        return fold(dot(hi, cat(list(b)), 1, 0)) + dot(lo, b[0], 1, 0)

    own_step = jnp.exp(jnp.broadcast_to(-rates[pos] * float(length), (1, HEAD_DIM)))
    own_group = jnp.exp(jnp.broadcast_to(-rates[pos] * float(length * heads), (1, HEAD_DIM)))

    def on_group(t, d, c, action):
        there = z + d if t == 0 else z - d
        ok = there < groups if t == 0 else there >= 0

        @pl.when(ok)
        def _():
            action(remote(
                gsend.at[t, c], ginbox.at[t, d - 1, c], gr_s.at[t, d - 1, c], gr_r.at[t, d - 1, c],
                seq=there * heads + pos,
            ))

    def direction(t):
        order = list(range(heads))
        return (order, ROWS, ROWS + 1) if t == 0 else (order[::-1], ROWS + 1, ROWS)

    def gather_group(t, c):
        inbox[t, pos, c] = loc[t, pos, c]
        for p in range(heads):
            @pl.when(p != pos)
            def _(p=p):
                remote(
                    loc.at[t, p, c], inbox.at[t, p, c], st_s.at[t, p, c], st_r.at[t, p, c], seq=base + p
                ).wait_recv()
        order, near, far = direction(t)
        total = None
        for i, p in enumerate(order):
            state = inbox[t, p, c, :ROWS]
            if i > 0:
                before = order[i - 1]
                keep = inbox[t, before, c, near : near + 1] == inbox[t, p, c, far : far + 1]
                came = jnp.where(keep, total, 0.0)
                csend[t, p, c] = came
                through = inbox[t, p, c, near : near + 1] == inbox[t, p, c, far : far + 1]
                total = state + jnp.where(through, own_step, 0.0) * came
            else:
                total = state
        gsend[t, c, :ROWS] = total
        gsend[t, c, ROWS:] = jnp.broadcast_to(inbox[t, order[-1], c, near : near + 1], (8, HEAD_DIM))
        for d in range(1, reach + 1):
            on_group(t, d, c, lambda copy: copy.start())

    def carry_out(t, c):
        order, near, far = direction(t)
        for d in range(1, reach + 1):
            there = z - d if t == 0 else z + d
            ok = there >= 0 if t == 0 else there < groups

            @pl.when(ok)
            def _(d=d):
                remote(
                    gsend.at[t, c], ginbox.at[t, d - 1, c], gr_s.at[t, d - 1, c], gr_r.at[t, d - 1, c],
                    seq=lax.rem(me + heads, n_seq),
                ).wait_recv()

            @pl.when(jnp.logical_not(ok))
            def _(d=d):
                ginbox[t, d - 1, c] = jnp.full((PAD, HEAD_DIM), -1.0, F32)
        enter = jnp.zeros((ROWS, HEAD_DIM), F32)
        factor = jnp.ones((1, HEAD_DIM), F32)
        for d in range(1, reach + 1):
            keep = ginbox[t, d - 1, c, ROWS : ROWS + 1] == inbox[t, order[0], c, far : far + 1]
            enter = enter + jnp.where(keep, factor, 0.0) * ginbox[t, d - 1, c, :ROWS]
            factor = factor * own_group
        factor = jnp.ones((1, HEAD_DIM), F32)
        for i, p in enumerate(order):
            if i == 0:
                csend[t, p, c] = enter
            else:
                before = order[i - 1]
                through = (
                    (inbox[t, before, c, near : near + 1] == inbox[t, p, c, far : far + 1])
                    & (inbox[t, before, c, near : near + 1] == inbox[t, before, c, far : far + 1])
                )
                factor = factor * jnp.where(through, own_step, 0.0)
                csend[t, p, c] = csend[t, p, c] + factor * enter
        for m in peers:
            remote(
                csend.at[t, m, c], carry.at[t, pos, c], ca_s.at[t, m, c], ca_r.at[t, pos, c], seq=base + m
            ).start()
        carry[t, pos, c] = csend[t, pos, c]

    def wait_carry(t, m):
        for c in range(CHUNKS):
            remote(
                csend.at[t, m, c], carry.at[t, m, c], ca_s.at[t, m, c], ca_r.at[t, m, c], seq=base + m
            ).wait_recv()

    def carried(t, h):
        return split(carry[t, h].reshape(HEAD_DIM, HEAD_DIM))

    def weave(work, steps, lead):
        rest = max(len(work) - lead, 1)
        done = 0
        for i, piece in enumerate(work):
            piece()
            due = (i + 1 - lead) * len(steps) // rest if i + 1 > lead else 0
            while done < min(due, len(steps)):
                steps[done]()
                done += 1
        while done < len(steps):
            steps[done]()
            done += 1

    def turn(h):
        q_t[h] = turned(q[h])

    def intra(h):
        out[h] = by_rows(a_hi[h], a_lo[h], split(v[h]))

    def each(f):
        return [functools.partial(f, h) for h in range(heads)]

    def chunks(f, t):
        return [functools.partial(f, t, c) for c in range(CHUNKS)]

    for h in range(heads):
        weigh(h)
    for h in range(heads):
        load(2, h).wait()
    weave(each(score) + each(turn) + each(intra), chunks(gather_group, 0) + chunks(carry_out, 0), 1)
    for h in range(heads):
        load(3, h).wait()
    def shape_grad(h):
        grad[h] = g[h] * gain_ref[:, lanes_of(h)]

    for h in range(heads):
        shape_grad(h)
    squares = jnp.zeros((length, HEAD_DIM), F32)
    product = jnp.zeros((length, HEAD_DIM), F32)
    for m in [pos] + peers[::-1]:
        if m is not pos:
            wait_carry(0, m)
        o = out[m] + cols[0, m] * square_by_rows(split(q[m]), carried(0, m))
        out[m] = o
        squares = squares + o * o
        product = product + grad[m] * o
    sums = cat([
        jnp.sum(squares.T, axis=0, keepdims=True),
        jnp.sum(product.T, axis=0, keepdims=True),
        jnp.zeros((6, length), F32),
    ], 0)
    hsend[...] = sums
    for o in range(1, n_head):
        other = lax.rem(hx + o, n_head)
        remote(hsend, hinbox.at[hx], hd_s.at[o], hd_r.at[hx], head=other).start()
    hinbox[hx] = sums
    for o in range(1, n_head):
        other = lax.rem(hx + o, n_head)
        remote(hsend, hinbox.at[other], hd_s.at[o], hd_r.at[other], head=other).wait_recv()
    sums = hinbox[0]
    for i in range(1, n_head):
        sums = sums + hinbox[i]
    inv_row = lax.rsqrt(sums[0:1] / features + EPSILON)
    coef_row = inv_row * inv_row * inv_row * (sums[1:2] / features)
    inv = jnp.broadcast_to(inv_row, (HEAD_DIM, length)).T
    coef = jnp.broadcast_to(coef_row, (HEAD_DIM, length)).T

    def local_back(m):
        o = out[m]
        d_out = inv * grad[m] - coef * o
        grad[m] = d_out
        back_w = jnp.exp(-rates[m] * place) * head_first
        part = jnp.sum(g[m] * o * inv, axis=0, keepdims=True)
        put(1, m, outer(q_t[m], d_out * back_w), jnp.where(row_id == 2, part, meta))

    for members in rounds:
        for m in members:
            local_back(m)
        post(1, members)
    local_back(pos)

    def group_gain():
        part = inbox[1, 0, 0, ROWS:]
        for p in range(1, heads):
            part = part + inbox[1, p, 0, ROWS:]
        nsend[...] = part
        ninbox[z] = part
        for o in range(1, groups):
            other = lax.rem(z + o, groups)
            remote(nsend, ninbox.at[z], ng_s.at[o], ng_r.at[z], seq=other * heads + pos).start()

    def whole_gain():
        for o in range(1, groups):
            other = lax.rem(z + o, groups)
            remote(nsend, ninbox.at[other], ng_s.at[o], ng_r.at[other], seq=other * heads + pos).wait_recv()
        part = ninbox[0]
        for i in range(1, groups):
            part = part + ninbox[i]
        tsend[...] = part
        tinbox[pos] = part
        for p in range(heads):
            @pl.when(p != pos)
            def _(p=p):
                remote(tsend, tinbox.at[pos], nt_s.at[p], nt_r.at[pos], seq=base + p).start()

    def for_queries(h):
        lanes = pl.ds(h * HEAD_DIM, HEAD_DIM)
        part = by_rows(p_hi[h], p_lo[h], split(k[h]))
        part = part + cols[0, h] * square_by_cols(split(grad[h]), carried(0, h))
        qg_ref[:, lanes] = part.astype(BF16)

    def for_keys(h):
        out[h] = under(q_t[h], p_hi[h], p_lo[h])

    def for_values(h):
        g[h] = under(turned(grad[h]), a_hi[h], a_lo[h])

    steps = chunks(gather_group, 1) + [group_gain] + chunks(carry_out, 1) + [whole_gain]
    weave(each(mix) + each(for_queries) + each(for_keys) + each(for_values), steps, heads)
    for m in [pos] + peers[::-1]:
        if m is not pos:
            wait_carry(1, m)
        state = carried(1, m)
        kg_ref[:, lanes_of(m)] = (out[m] + cols[1, m] * square_by_cols(split(v[m]), state)).astype(BF16)
        vg_ref[:, lanes_of(m)] = (g[m] + cols[1, m] * square_by_rows(split(k[m]), state)).astype(BF16)
    for p in range(heads):
        @pl.when(p != pos)
        def _(p=p):
            remote(tsend, tinbox.at[p], nt_s.at[p], nt_r.at[p], seq=base + p).wait_recv()
    for h in range(heads):
        gain_out[:, h * HEAD_DIM : (h + 1) * HEAD_DIM] = tinbox[h, 2:3]

    for t in range(2):
        for c in range(CHUNKS):
            for m in peers:
                remote(
                    loc.at[t, m, c], inbox.at[t, pos, c], st_s.at[t, m, c], st_r.at[t, pos, c], seq=base + m
                ).wait_send()
                remote(
                    csend.at[t, m, c], carry.at[t, pos, c], ca_s.at[t, m, c], ca_r.at[t, pos, c], seq=base + m
                ).wait_send()
            for d in range(1, reach + 1):
                on_group(t, d, c, lambda copy: copy.wait_send())
    for o in range(1, n_head):
        remote(hsend, hinbox.at[hx], hd_s.at[o], hd_r.at[hx], head=lax.rem(hx + o, n_head)).wait_send()
    for o in range(1, groups):
        other = lax.rem(z + o, groups)
        remote(nsend, ninbox.at[z], ng_s.at[o], ng_r.at[z], seq=other * heads + pos).wait_send()
    for p in range(heads):
        @pl.when(p != pos)
        def _(p=p):
            remote(tsend, tinbox.at[pos], nt_s.at[p], nt_r.at[pos], seq=base + p).wait_send()


def store(*refs):
    sem = refs[-1]
    copies = [pltpu.make_async_copy(refs[i], refs[4 + i], sem.at[i]) for i in range(4)]
    for copy in copies:
        copy.start()
    for copy in copies:
        copy.wait()


def body(n_seq, n_head, queries, key_vectors, value_vectors, out_grad, norm_gain, decay_rates, segment_ids):
    length, width = queries.shape
    heads = width // HEAD_DIM
    groups = n_seq // heads
    longest = (length * n_seq) // 3
    blocks = -(-(longest - 1) // length)
    reach = min(-(-blocks // heads), groups - 1)
    shape = (heads, length, n_seq, n_head, groups, reach)
    any_spec = pl.BlockSpec(memory_space=pl.ANY)
    vmem = pl.BlockSpec(memory_space=pltpu.VMEM)
    tok = (heads, length, HEAD_DIM)
    sq = (heads, length, length)
    dma = pltpu.SemaphoreType.DMA
    outs = pl.pallas_call(
        functools.partial(kernel, shape),
        out_shape=(
            jax.ShapeDtypeStruct((length, width), BF16),
            jax.ShapeDtypeStruct((length, width), BF16),
            jax.ShapeDtypeStruct((length, width), BF16),
            jax.ShapeDtypeStruct((1, width), F32),
        ),
        in_specs=[any_spec] * 4 + [vmem, pl.BlockSpec(memory_space=pltpu.SMEM), vmem],
        out_specs=(vmem,) * 4,
        scratch_shapes=[
            pltpu.VMEM(tok, F32), pltpu.VMEM(tok, F32), pltpu.VMEM(tok, F32), pltpu.VMEM(tok, F32),
            pltpu.VMEM(sq, F32),
            pltpu.VMEM(sq, BF16), pltpu.VMEM(sq, BF16), pltpu.VMEM(sq, BF16), pltpu.VMEM(sq, BF16),
            pltpu.VMEM(tok, F32), pltpu.VMEM(tok, F32),
            pltpu.VMEM((2,) + tok, F32),
            pltpu.VMEM((heads, 2 * HEAD_DIM, length), BF16),
            pltpu.VMEM((2, heads, CHUNKS, PAD, HEAD_DIM), F32),
            pltpu.VMEM((2, heads, CHUNKS, PAD, HEAD_DIM), F32),
            pltpu.VMEM((2, CHUNKS, PAD, HEAD_DIM), F32),
            pltpu.VMEM((2, reach, CHUNKS, PAD, HEAD_DIM), F32),
            pltpu.VMEM((2, heads, CHUNKS, ROWS, HEAD_DIM), F32),
            pltpu.VMEM((2, heads, CHUNKS, ROWS, HEAD_DIM), F32),
            pltpu.VMEM((8, length), F32),
            pltpu.VMEM((n_head, 8, length), F32),
            pltpu.VMEM((8, HEAD_DIM), F32),
            pltpu.VMEM((groups, 8, HEAD_DIM), F32),
            pltpu.VMEM((8, HEAD_DIM), F32),
            pltpu.VMEM((heads, 8, HEAD_DIM), F32),
            dma((4, heads)),
            dma((2, heads, CHUNKS)), dma((2, heads, CHUNKS)),
            dma((2, reach, CHUNKS)), dma((2, reach, CHUNKS)),
            dma((2, heads, CHUNKS)), dma((2, heads, CHUNKS)),
            dma((n_head,)), dma((n_head,)),
            dma((groups,)), dma((groups,)),
            dma((heads,)), dma((heads,)),
        ],
        compiler_params=pltpu.CompilerParams(
            collective_id=0, has_side_effects=True, vmem_limit_bytes=VMEM_BYTES
        ),
        name="decayed_attention_grad",
    )(
        queries, key_vectors, value_vectors, out_grad,
        norm_gain.reshape(1, width), decay_rates, segment_ids,
    )
    outs = pl.pallas_call(
        store,
        out_shape=tuple(jax.ShapeDtypeStruct(x.shape, x.dtype) for x in outs),
        in_specs=[vmem] * 4,
        out_specs=(any_spec,) * 4,
        scratch_shapes=[dma((4,))],
        compiler_params=pltpu.CompilerParams(vmem_limit_bytes=VMEM_BYTES),
        name="store_results",
    )(*outs)
    return outs[0], outs[1], outs[2], outs[3].reshape(width)


def solution(mesh):
    return jax.shard_map(
        functools.partial(body, mesh.shape["seq"], mesh.shape["head"]),
        mesh=mesh,
        in_specs=(
            P("seq", "head"),
            P("seq", "head"),
            P("seq", "head"),
            P("seq", "head"),
            P("head"),
            P("head"),
            P("seq"),
        ),
        out_specs=(P("seq", "head"), P("seq", "head"), P("seq", "head"), P("head")),
        check_vma=False,
    )
```

```python
import functools

import jax
import jax.numpy as jnp
from jax import lax
from jax.experimental import pallas as pl
from jax.experimental.pallas import tpu as pltpu
from jax.sharding import PartitionSpec as P

HEAD_DIM = 128
CHUNKS = 2
ROWS = HEAD_DIM // CHUNKS
PAD = ROWS + 8
CORES = 2
GROUP = 256
VMEM_BYTES = 63 * 1024 * 1024
EPSILON = 1e-06
F32 = jnp.float32
BF16 = jnp.bfloat16


def split(x):
    hi = x.astype(BF16)
    return hi, (x - hi.astype(F32)).astype(BF16)


def dot(a, b, ca, cb):
    return lax.dot_general(a, b, (((ca,), (cb,)), ((), ())), preferred_element_type=F32)


def cat(parts, axis=1):
    return jnp.concatenate(parts, axis=axis)


def rows_by_rows(a, b):
    return dot(cat([a[0], a[1], a[0]]), cat([b[0], b[0], b[1]]), 1, 1)


def fold(both):
    return both[:, :HEAD_DIM] + both[:, HEAD_DIM:]


def square_by_rows(a, b):
    half = cat([b[0], b[1]])
    return fold(dot(cat(list(a)), cat([half, half], 0), 1, 0))


def square_by_cols(a, b):
    half = cat([b[0], b[1]], 0)
    return fold(dot(cat(list(a)), cat([half, half]), 1, 1))


def turned(x):
    return cat(list(split(x.T)), 0)


def outer(a_t, b):
    both = fold(dot(a_t, cat(list(split(b))), 1, 0))
    return both[:HEAD_DIM] + both[HEAD_DIM:]


def column_groups(length):
    return [(j, min(j + GROUP, length)) for j in range(0, length, GROUP)]


def under(a_t, hi, lo, h):
    length = hi.shape[1]
    parts = []
    for j, end in column_groups(length):
        both = dot(a_t[:, j:], hi[h, j:, j:end], 1, 0)
        part = both[:HEAD_DIM] + both[HEAD_DIM:] + dot(a_t[:HEAD_DIM, j:], lo[h, j:, j:end], 1, 0)
        parts.append(part.T)
    return cat(parts, 0)


def by_rows(hi, lo, h, b):
    length = hi.shape[1]
    both = cat(list(b))
    total = None
    for j, end in column_groups(length):
        part = fold(dot(hi[h, j:, j:end], both[j:end], 1, 0)) + dot(lo[h, j:, j:end], b[0][j:end], 1, 0)
        total = part if total is None else cat([total[:j], total[j:] + part], 0)
    return total


def triangle(hi, lo, h, a, b, w):
    length = hi.shape[1]
    for j, end in column_groups(length):
        part = rows_by_rows([x[j:] for x in a], [x[j:end] for x in b]) * w[h, j:, j:end]
        hi[h, j:, j:end], lo[h, j:, j:end] = split(part)


def kernel(
    shape, q_hbm, k_hbm, v_hbm, g_hbm, gain_ref, rates, seg_ref,
    qg_ref, kg_ref, vg_ref, gain_out,
    q, k, v, g, w, a_hi, a_lo, p_hi, p_lo, out, grad, cols, q_t,
    loc, inbox, gsend, ginbox, csend, carry,
    hsend, hinbox, nsend, ninbox, tsend, tinbox,
    in_sem, st_s, st_r, gr_s, gr_r, ca_s, ca_r, hd_s, hd_r, ng_s, ng_r, nt_s, nt_r,
):
    heads, length, n_seq, n_head, groups, reach = shape
    me = lax.axis_index("seq")
    hx = lax.axis_index("head")
    pos = lax.rem(me, heads)
    z = lax.div(me, heads)
    base = z * heads
    features = float(heads * HEAD_DIM * n_head)

    def lanes_of(h):
        return pl.ds(pl.multiple_of(h * HEAD_DIM, HEAD_DIM), HEAD_DIM)

    def load(i, h):
        src, dst = ((k_hbm, k), (v_hbm, v), (q_hbm, q), (g_hbm, g))[i]
        return pltpu.make_async_copy(
            src.at[:, lanes_of(h)], dst.at[h], in_sem.at[i, h]
        )

    side = lax.div(pos, CORES)
    sides = heads // CORES

    def others(o):
        there = lax.rem(side + o, sides) * CORES
        return [there + i for i in range(CORES)]

    mates = [side * CORES + lax.rem(pos - side * CORES + i, CORES) for i in range(1, CORES)]
    rounds = [others(o) for o in range(1, sides)] + [mates]
    peers = [m for members in rounds for m in members]

    for m in peers + [pos]:
        load(0, m).start()
        load(1, m).start()
    for i in (2, 3):
        for m in range(heads):
            load(i, m).start()

    def remote(src, dst, ss, rs, **where):
        return pltpu.make_async_remote_copy(
            src_ref=src, dst_ref=dst, send_sem=ss, recv_sem=rs,
            device_id=where, device_id_type=pl.DeviceIdType.MESH,
        )

    barrier = pltpu.get_barrier_semaphore()

    def greet(**where):
        pl.semaphore_signal(barrier, inc=1, device_id=where, device_id_type=pl.DeviceIdType.MESH)

    for o in range(1, heads):
        greet(seq=base + lax.rem(pos + o, heads))
    for o in range(1, groups):
        greet(seq=lax.rem(z + o, groups) * heads + pos)
    for o in range(1, n_head):
        greet(head=lax.rem(hx + o, n_head))

    seg_row = seg_ref[...].reshape(1, length).astype(F32)
    first = seg_row[0:1, 0:1]
    last = seg_row[0:1, length - 1 : length]
    seg_col = jnp.broadcast_to(seg_row, (HEAD_DIM, length)).T
    place = lax.broadcasted_iota(jnp.int32, (length, HEAD_DIM), 0).astype(F32)
    head_first = jnp.where(seg_col == first, 1.0, 0.0)
    tail_last = jnp.where(seg_col == last, 1.0, 0.0)
    for h in range(heads):
        rate = rates[h]
        cols[0, h] = jnp.exp(-rate * (place + 1.0)) * head_first
        cols[1, h] = jnp.exp(-rate * (length - place)) * tail_last

    def post(t, members):
        for c in range(CHUNKS):
            for m in members:
                remote(
                    loc.at[t, m, c], inbox.at[t, pos, c], st_s.at[t, m, c], st_r.at[t, pos, c], seq=base + m
                ).start()

    def put(t, m, state, tail):
        for c in range(CHUNKS):
            loc[t, m, c, :ROWS] = state[c * ROWS : (c + 1) * ROWS]
            loc[t, m, c, ROWS:] = tail

    row_id = lax.broadcasted_iota(jnp.int32, (8, HEAD_DIM), 0)
    meta = jnp.where(row_id == 0, last, jnp.where(row_id == 1, first, 0.0))

    def local_state(m):
        load(0, m).wait()
        load(1, m).wait()
        out_w = jnp.exp(-rates[m] * (length - 1.0 - place)) * tail_last
        put(0, m, outer(turned(k[m]), v[m] * out_w), meta)

    for i, members in enumerate(rounds):
        for m in members:
            local_state(m)
        if i == 0:
            pl.semaphore_wait(barrier, (heads - 1) + (groups - 1) + (n_head - 1))
        post(0, members)
    local_state(pos)

    cell_gap = (
        lax.broadcasted_iota(jnp.int32, (HEAD_DIM, HEAD_DIM), 0)
        - lax.broadcasted_iota(jnp.int32, (HEAD_DIM, HEAD_DIM), 1)
    ).astype(F32)

    def weigh(h):
        rate = rates[h]
        near_w = jnp.where(cell_gap >= 0.0, jnp.exp(-rate * jnp.maximum(cell_gap, 0.0)), 0.0)
        far_w = jnp.exp(-rate * (cell_gap + float(HEAD_DIM)))
        step = jnp.exp(jnp.broadcast_to(-rate * float(HEAD_DIM), (1, HEAD_DIM)))
        factors = []
        for _ in range(1, length // HEAD_DIM):
            factors.append(far_w)
            far_w = far_w * step
        for j, end in column_groups(length):
            for r in range(j, length, HEAD_DIM):
                for c in range(j, end, HEAD_DIM):
                    cell = jnp.zeros((HEAD_DIM, HEAD_DIM), F32)
                    if r >= c:
                        value = near_w if r == c else factors[(r - c) // HEAD_DIM - 1]
                        same = seg_col[r : r + HEAD_DIM] == seg_row[:, c : c + HEAD_DIM]
                        cell = jnp.where(same, value, 0.0)
                    w[h, r : r + HEAD_DIM, c : c + HEAD_DIM] = cell

    def score(h):
        triangle(a_hi, a_lo, h, split(q[h]), split(k[h]), w)

    def mix(h):
        triangle(p_hi, p_lo, h, split(grad[h]), split(v[h]), w)

    own_step = jnp.exp(jnp.broadcast_to(-rates[pos] * float(length), (1, HEAD_DIM)))
    own_group = jnp.exp(jnp.broadcast_to(-rates[pos] * float(length * heads), (1, HEAD_DIM)))

    def on_group(t, d, c, action):
        there = z + d if t == 0 else z - d
        ok = there < groups if t == 0 else there >= 0

        @pl.when(ok)
        def _():
            action(remote(
                gsend.at[t, c], ginbox.at[t, d - 1, c], gr_s.at[t, d - 1, c], gr_r.at[t, d - 1, c],
                seq=there * heads + pos,
            ))

    def direction(t):
        order = list(range(heads))
        return (order, ROWS, ROWS + 1) if t == 0 else (order[::-1], ROWS + 1, ROWS)

    def gather_group(t, c):
        inbox[t, pos, c] = loc[t, pos, c]
        for p in range(heads):
            @pl.when(p != pos)
            def _(p=p):
                remote(
                    loc.at[t, p, c], inbox.at[t, p, c], st_s.at[t, p, c], st_r.at[t, p, c], seq=base + p
                ).wait_recv()
        order, near, far = direction(t)
        total = None
        for i, p in enumerate(order):
            state = inbox[t, p, c, :ROWS]
            if i > 0:
                before = order[i - 1]
                keep = inbox[t, before, c, near : near + 1] == inbox[t, p, c, far : far + 1]
                came = jnp.where(keep, total, 0.0)
                csend[t, p, c] = came
                through = inbox[t, p, c, near : near + 1] == inbox[t, p, c, far : far + 1]
                total = state + jnp.where(through, own_step, 0.0) * came
            else:
                total = state
        gsend[t, c, :ROWS] = total
        gsend[t, c, ROWS:] = jnp.broadcast_to(inbox[t, order[-1], c, near : near + 1], (8, HEAD_DIM))
        for d in range(1, reach + 1):
            on_group(t, d, c, lambda copy: copy.start())

    def carry_out(t, c):
        order, near, far = direction(t)
        for d in range(1, reach + 1):
            there = z - d if t == 0 else z + d
            ok = there >= 0 if t == 0 else there < groups

            @pl.when(ok)
            def _(d=d):
                remote(
                    gsend.at[t, c], ginbox.at[t, d - 1, c], gr_s.at[t, d - 1, c], gr_r.at[t, d - 1, c],
                    seq=lax.rem(me + heads, n_seq),
                ).wait_recv()

            @pl.when(jnp.logical_not(ok))
            def _(d=d):
                ginbox[t, d - 1, c] = jnp.full((PAD, HEAD_DIM), -1.0, F32)
        enter = jnp.zeros((ROWS, HEAD_DIM), F32)
        factor = jnp.ones((1, HEAD_DIM), F32)
        for d in range(1, reach + 1):
            keep = ginbox[t, d - 1, c, ROWS : ROWS + 1] == inbox[t, order[0], c, far : far + 1]
            enter = enter + jnp.where(keep, factor, 0.0) * ginbox[t, d - 1, c, :ROWS]
            factor = factor * own_group
        factor = jnp.ones((1, HEAD_DIM), F32)
        for i, p in enumerate(order):
            if i == 0:
                csend[t, p, c] = enter
            else:
                before = order[i - 1]
                through = (
                    (inbox[t, before, c, near : near + 1] == inbox[t, p, c, far : far + 1])
                    & (inbox[t, before, c, near : near + 1] == inbox[t, before, c, far : far + 1])
                )
                factor = factor * jnp.where(through, own_step, 0.0)
                csend[t, p, c] = csend[t, p, c] + factor * enter
        for m in peers:
            remote(
                csend.at[t, m, c], carry.at[t, pos, c], ca_s.at[t, m, c], ca_r.at[t, pos, c], seq=base + m
            ).start()
        carry[t, pos, c] = csend[t, pos, c]

    def wait_carry(t, m):
        for c in range(CHUNKS):
            remote(
                csend.at[t, m, c], carry.at[t, m, c], ca_s.at[t, m, c], ca_r.at[t, m, c], seq=base + m
            ).wait_recv()

    def carried(t, h):
        return split(carry[t, h].reshape(HEAD_DIM, HEAD_DIM))

    def weave(work, steps, lead):
        rest = max(len(work) - lead, 1)
        done = 0
        for i, piece in enumerate(work):
            piece()
            due = (i + 1 - lead) * len(steps) // rest if i + 1 > lead else 0
            while done < min(due, len(steps)):
                steps[done]()
                done += 1
        while done < len(steps):
            steps[done]()
            done += 1

    def turn(h):
        q_t[h] = turned(q[h])

    def intra(h):
        out[h] = by_rows(a_hi, a_lo, h, split(v[h]))

    def each(f):
        return [functools.partial(f, h) for h in range(heads)]

    def chunks(f, t):
        return [functools.partial(f, t, c) for c in range(CHUNKS)]

    for h in range(heads):
        weigh(h)
    for h in range(heads):
        load(2, h).wait()
    weave(each(score) + each(turn) + each(intra), chunks(gather_group, 0) + chunks(carry_out, 0), 1)
    for h in range(heads):
        load(3, h).wait()
    def shape_grad(h):
        grad[h] = g[h] * gain_ref[:, lanes_of(h)]

    for h in range(heads):
        shape_grad(h)
    squares = jnp.zeros((length, HEAD_DIM), F32)
    product = jnp.zeros((length, HEAD_DIM), F32)
    for m in [pos] + peers[::-1]:
        if m is not pos:
            wait_carry(0, m)
        o = out[m] + cols[0, m] * square_by_rows(split(q[m]), carried(0, m))
        out[m] = o
        squares = squares + o * o
        product = product + grad[m] * o
    sums = cat([
        jnp.sum(squares.T, axis=0, keepdims=True),
        jnp.sum(product.T, axis=0, keepdims=True),
        jnp.zeros((6, length), F32),
    ], 0)
    hsend[...] = sums
    for o in range(1, n_head):
        other = lax.rem(hx + o, n_head)
        remote(hsend, hinbox.at[hx], hd_s.at[o], hd_r.at[hx], head=other).start()
    hinbox[hx] = sums
    for o in range(1, n_head):
        other = lax.rem(hx + o, n_head)
        remote(hsend, hinbox.at[other], hd_s.at[o], hd_r.at[other], head=other).wait_recv()
    sums = hinbox[0]
    for i in range(1, n_head):
        sums = sums + hinbox[i]
    inv_row = lax.rsqrt(sums[0:1] / features + EPSILON)
    coef_row = inv_row * inv_row * inv_row * (sums[1:2] / features)
    inv = jnp.broadcast_to(inv_row, (HEAD_DIM, length)).T
    coef = jnp.broadcast_to(coef_row, (HEAD_DIM, length)).T

    def local_back(m):
        o = out[m]
        d_out = inv * grad[m] - coef * o
        grad[m] = d_out
        back_w = jnp.exp(-rates[m] * place) * head_first
        part = jnp.sum(g[m] * o * inv, axis=0, keepdims=True)
        put(1, m, outer(q_t[m], d_out * back_w), jnp.where(row_id == 2, part, meta))

    for members in rounds:
        for m in members:
            local_back(m)
        post(1, members)
    local_back(pos)

    def group_gain():
        part = inbox[1, 0, 0, ROWS:]
        for p in range(1, heads):
            part = part + inbox[1, p, 0, ROWS:]
        nsend[...] = part
        ninbox[z] = part
        for o in range(1, groups):
            other = lax.rem(z + o, groups)
            remote(nsend, ninbox.at[z], ng_s.at[o], ng_r.at[z], seq=other * heads + pos).start()

    def whole_gain():
        for o in range(1, groups):
            other = lax.rem(z + o, groups)
            remote(nsend, ninbox.at[other], ng_s.at[o], ng_r.at[other], seq=other * heads + pos).wait_recv()
        part = ninbox[0]
        for i in range(1, groups):
            part = part + ninbox[i]
        tsend[...] = part
        tinbox[pos] = part
        for p in range(heads):
            @pl.when(p != pos)
            def _(p=p):
                remote(tsend, tinbox.at[pos], nt_s.at[p], nt_r.at[pos], seq=base + p).start()

    def for_queries(h):
        lanes = pl.ds(h * HEAD_DIM, HEAD_DIM)
        part = by_rows(p_hi, p_lo, h, split(k[h]))
        part = part + cols[0, h] * square_by_cols(split(grad[h]), carried(0, h))
        qg_ref[:, lanes] = part.astype(BF16)

    def for_keys(h):
        out[h] = under(q_t[h], p_hi, p_lo, h)

    def for_values(h):
        g[h] = under(turned(grad[h]), a_hi, a_lo, h)

    steps = chunks(gather_group, 1) + [group_gain] + chunks(carry_out, 1) + [whole_gain]
    weave(each(mix) + each(for_queries) + each(for_keys) + each(for_values), steps, heads)
    for m in [pos] + peers[::-1]:
        if m is not pos:
            wait_carry(1, m)
        state = carried(1, m)
        kg_ref[:, lanes_of(m)] = (out[m] + cols[1, m] * square_by_cols(split(v[m]), state)).astype(BF16)
        vg_ref[:, lanes_of(m)] = (g[m] + cols[1, m] * square_by_rows(split(k[m]), state)).astype(BF16)
    for p in range(heads):
        @pl.when(p != pos)
        def _(p=p):
            remote(tsend, tinbox.at[p], nt_s.at[p], nt_r.at[p], seq=base + p).wait_recv()
    for h in range(heads):
        gain_out[:, h * HEAD_DIM : (h + 1) * HEAD_DIM] = tinbox[h, 2:3]

    for t in range(2):
        for c in range(CHUNKS):
            for m in peers:
                remote(
                    loc.at[t, m, c], inbox.at[t, pos, c], st_s.at[t, m, c], st_r.at[t, pos, c], seq=base + m
                ).wait_send()
                remote(
                    csend.at[t, m, c], carry.at[t, pos, c], ca_s.at[t, m, c], ca_r.at[t, pos, c], seq=base + m
                ).wait_send()
            for d in range(1, reach + 1):
                on_group(t, d, c, lambda copy: copy.wait_send())
    for o in range(1, n_head):
        remote(hsend, hinbox.at[hx], hd_s.at[o], hd_r.at[hx], head=lax.rem(hx + o, n_head)).wait_send()
    for o in range(1, groups):
        other = lax.rem(z + o, groups)
        remote(nsend, ninbox.at[z], ng_s.at[o], ng_r.at[z], seq=other * heads + pos).wait_send()
    for p in range(heads):
        @pl.when(p != pos)
        def _(p=p):
            remote(tsend, tinbox.at[pos], nt_s.at[p], nt_r.at[pos], seq=base + p).wait_send()


def store(*refs):
    sem = refs[-1]
    copies = [pltpu.make_async_copy(refs[i], refs[4 + i], sem.at[i]) for i in range(4)]
    for copy in copies:
        copy.start()
    for copy in copies:
        copy.wait()


def body(n_seq, n_head, queries, key_vectors, value_vectors, out_grad, norm_gain, decay_rates, segment_ids):
    length, width = queries.shape
    heads = width // HEAD_DIM
    groups = n_seq // heads
    longest = (length * n_seq) // 3
    blocks = -(-(longest - 1) // length)
    reach = min(-(-blocks // heads), groups - 1)
    shape = (heads, length, n_seq, n_head, groups, reach)
    any_spec = pl.BlockSpec(memory_space=pl.ANY)
    vmem = pl.BlockSpec(memory_space=pltpu.VMEM)
    tok = (heads, length, HEAD_DIM)
    sq = (heads, length, length)
    dma = pltpu.SemaphoreType.DMA
    outs = pl.pallas_call(
        functools.partial(kernel, shape),
        out_shape=(
            jax.ShapeDtypeStruct((length, width), BF16),
            jax.ShapeDtypeStruct((length, width), BF16),
            jax.ShapeDtypeStruct((length, width), BF16),
            jax.ShapeDtypeStruct((1, width), F32),
        ),
        in_specs=[any_spec] * 4 + [vmem, pl.BlockSpec(memory_space=pltpu.SMEM), vmem],
        out_specs=(vmem,) * 4,
        scratch_shapes=[
            pltpu.VMEM(tok, F32), pltpu.VMEM(tok, F32), pltpu.VMEM(tok, F32), pltpu.VMEM(tok, F32),
            pltpu.VMEM(sq, F32),
            pltpu.VMEM(sq, BF16), pltpu.VMEM(sq, BF16), pltpu.VMEM(sq, BF16), pltpu.VMEM(sq, BF16),
            pltpu.VMEM(tok, F32), pltpu.VMEM(tok, F32),
            pltpu.VMEM((2,) + tok, F32),
            pltpu.VMEM((heads, 2 * HEAD_DIM, length), BF16),
            pltpu.VMEM((2, heads, CHUNKS, PAD, HEAD_DIM), F32),
            pltpu.VMEM((2, heads, CHUNKS, PAD, HEAD_DIM), F32),
            pltpu.VMEM((2, CHUNKS, PAD, HEAD_DIM), F32),
            pltpu.VMEM((2, reach, CHUNKS, PAD, HEAD_DIM), F32),
            pltpu.VMEM((2, heads, CHUNKS, ROWS, HEAD_DIM), F32),
            pltpu.VMEM((2, heads, CHUNKS, ROWS, HEAD_DIM), F32),
            pltpu.VMEM((8, length), F32),
            pltpu.VMEM((n_head, 8, length), F32),
            pltpu.VMEM((8, HEAD_DIM), F32),
            pltpu.VMEM((groups, 8, HEAD_DIM), F32),
            pltpu.VMEM((8, HEAD_DIM), F32),
            pltpu.VMEM((heads, 8, HEAD_DIM), F32),
            dma((4, heads)),
            dma((2, heads, CHUNKS)), dma((2, heads, CHUNKS)),
            dma((2, reach, CHUNKS)), dma((2, reach, CHUNKS)),
            dma((2, heads, CHUNKS)), dma((2, heads, CHUNKS)),
            dma((n_head,)), dma((n_head,)),
            dma((groups,)), dma((groups,)),
            dma((heads,)), dma((heads,)),
        ],
        compiler_params=pltpu.CompilerParams(
            collective_id=0, has_side_effects=True, vmem_limit_bytes=VMEM_BYTES
        ),
        name="decayed_attention_grad",
    )(
        queries, key_vectors, value_vectors, out_grad,
        norm_gain.reshape(1, width), decay_rates, segment_ids,
    )
    outs = pl.pallas_call(
        store,
        out_shape=tuple(jax.ShapeDtypeStruct(x.shape, x.dtype) for x in outs),
        in_specs=[vmem] * 4,
        out_specs=(any_spec,) * 4,
        scratch_shapes=[dma((4,))],
        compiler_params=pltpu.CompilerParams(vmem_limit_bytes=VMEM_BYTES),
        name="store_results",
    )(*outs)
    return outs[0], outs[1], outs[2], outs[3].reshape(width)


def solution(mesh):
    return jax.shard_map(
        functools.partial(body, mesh.shape["seq"], mesh.shape["head"]),
        mesh=mesh,
        in_specs=(
            P("seq", "head"),
            P("seq", "head"),
            P("seq", "head"),
            P("seq", "head"),
            P("head"),
            P("head"),
            P("seq"),
        ),
        out_specs=(P("seq", "head"), P("seq", "head"), P("seq", "head"), P("head")),
        check_vma=False,
    )
```

```python
import functools

import jax
import jax.numpy as jnp
from jax import lax
from jax.experimental import pallas as pl
from jax.experimental.pallas import tpu as pltpu
from jax.sharding import PartitionSpec as P

HEAD_DIM = 128
CHUNKS = 2
ROWS = HEAD_DIM // CHUNKS
PAD = ROWS + 8
CORES = 2
GROUP = 256
VMEM_BYTES = 63 * 1024 * 1024
EPSILON = 1e-06
F32 = jnp.float32
BF16 = jnp.bfloat16


def split(x):
    hi = x.astype(BF16)
    return hi, (x - hi.astype(F32)).astype(BF16)


def dot(a, b, ca, cb):
    return lax.dot_general(a, b, (((ca,), (cb,)), ((), ())), preferred_element_type=F32)


def cat(parts, axis=1):
    return jnp.concatenate(parts, axis=axis)


def rows_by_rows(a, b):
    return dot(cat([a[0], a[1], a[0]]), cat([b[0], b[0], b[1]]), 1, 1)


def fold(both):
    return both[:, :HEAD_DIM] + both[:, HEAD_DIM:]


def square_by_rows(a, b):
    half = cat([b[0], b[1]])
    return fold(dot(cat(list(a)), cat([half, half], 0), 1, 0))


def square_by_cols(a, b):
    half = cat([b[0], b[1]], 0)
    return fold(dot(cat(list(a)), cat([half, half]), 1, 1))


def turned(x):
    return cat(list(split(x.T)), 0)


def outer(a_t, b):
    both = fold(dot(a_t, cat(list(split(b))), 1, 0))
    return both[:HEAD_DIM] + both[HEAD_DIM:]


def column_groups(length):
    return [(j, min(j + GROUP, length)) for j in range(0, length, GROUP)]


def under(a_t, hi, lo, h):
    length = hi.shape[1]
    parts = []
    for j, end in column_groups(length):
        both = dot(a_t[:, j:], hi[h, j:, j:end], 1, 0)
        part = both[:HEAD_DIM] + both[HEAD_DIM:] + dot(a_t[:HEAD_DIM, j:], lo[h, j:, j:end], 1, 0)
        parts.append(part.T)
    return cat(parts, 0)


def by_rows(hi, lo, h, b):
    length = hi.shape[1]
    both = cat(list(b))
    total = None
    for j, end in column_groups(length):
        part = fold(dot(hi[h, j:, j:end], both[j:end], 1, 0)) + dot(lo[h, j:, j:end], b[0][j:end], 1, 0)
        total = part if total is None else cat([total[:j], total[j:] + part], 0)
    return total


def triangle(hi, lo, h, a, b, w):
    length = hi.shape[1]
    for j, end in column_groups(length):
        part = rows_by_rows([x[j:] for x in a], [x[j:end] for x in b]) * w[h, j:, j:end]
        hi[h, j:, j:end], lo[h, j:, j:end] = split(part)


def kernel(
    shape, q_hbm, k_hbm, v_hbm, g_hbm, gain_ref, rates, seg_ref,
    qg_ref, kg_ref, vg_ref, gain_out,
    q, k, v, g, w, a_hi, a_lo, p_hi, p_lo, out, grad, cols, q_t,
    loc, inbox, gsend, ginbox, csend, carry,
    hsend, hinbox, ninbox, tsend, tinbox,
    in_sem, st_s, st_r, gr_s, gr_r, ca_s, ca_r, hd_s, hd_r, ng_s, ng_r, nt_s, nt_r,
):
    heads, length, n_seq, n_head, groups, reach = shape
    me = lax.axis_index("seq")
    hx = lax.axis_index("head")
    pos = lax.rem(me, heads)
    z = lax.div(me, heads)
    base = z * heads
    features = float(heads * HEAD_DIM * n_head)

    def lanes_of(h):
        return pl.ds(pl.multiple_of(h * HEAD_DIM, HEAD_DIM), HEAD_DIM)

    def load(i, h):
        src, dst = ((k_hbm, k), (v_hbm, v), (q_hbm, q), (g_hbm, g))[i]
        return pltpu.make_async_copy(
            src.at[:, lanes_of(h)], dst.at[h], in_sem.at[i, h]
        )

    side = lax.div(pos, CORES)
    sides = heads // CORES

    def others(o):
        there = lax.rem(side + o, sides) * CORES
        return [there + i for i in range(CORES)]

    mates = [side * CORES + lax.rem(pos - side * CORES + i, CORES) for i in range(1, CORES)]
    rounds = [others(o) for o in range(1, sides)] + [mates]
    peers = [m for members in rounds for m in members]

    for m in peers + [pos]:
        load(0, m).start()
        load(1, m).start()
    for i in (2, 3):
        for m in range(heads):
            load(i, m).start()

    def remote(src, dst, ss, rs, **where):
        return pltpu.make_async_remote_copy(
            src_ref=src, dst_ref=dst, send_sem=ss, recv_sem=rs,
            device_id=where, device_id_type=pl.DeviceIdType.MESH,
        )

    barrier = pltpu.get_barrier_semaphore()

    def greet(**where):
        pl.semaphore_signal(barrier, inc=1, device_id=where, device_id_type=pl.DeviceIdType.MESH)

    for o in range(1, heads):
        greet(seq=base + lax.rem(pos + o, heads))
    for d in range(1, reach + 1):
        @pl.when(z >= d)
        def _(d=d):
            greet(seq=me - d * heads)

        @pl.when(z + d < groups)
        def _(d=d):
            greet(seq=me + d * heads)

    for o in range(1, n_head):
        greet(head=lax.rem(hx + o, n_head))

    seg_row = seg_ref[...].reshape(1, length).astype(F32)
    first = seg_row[0:1, 0:1]
    last = seg_row[0:1, length - 1 : length]
    seg_col = jnp.broadcast_to(seg_row, (HEAD_DIM, length)).T
    place = lax.broadcasted_iota(jnp.int32, (length, HEAD_DIM), 0).astype(F32)
    head_first = jnp.where(seg_col == first, 1.0, 0.0)
    tail_last = jnp.where(seg_col == last, 1.0, 0.0)
    for h in range(heads):
        rate = rates[h]
        cols[0, h] = jnp.exp(-rate * (place + 1.0)) * head_first
        cols[1, h] = jnp.exp(-rate * (length - place)) * tail_last

    def post(t, members):
        for c in range(CHUNKS):
            for m in members:
                remote(
                    loc.at[t, m, c], inbox.at[t, pos, c], st_s.at[t, m, c], st_r.at[t, pos, c], seq=base + m
                ).start()

    def put(t, m, state, tail):
        for c in range(CHUNKS):
            loc[t, m, c, :ROWS] = state[c * ROWS : (c + 1) * ROWS]
            loc[t, m, c, ROWS:] = tail

    row_id = lax.broadcasted_iota(jnp.int32, (8, HEAD_DIM), 0)
    meta = jnp.where(row_id == 0, last, jnp.where(row_id == 1, first, 0.0))

    def local_state(m):
        load(0, m).wait()
        load(1, m).wait()
        out_w = jnp.exp(-rates[m] * (length - 1.0 - place)) * tail_last
        put(0, m, outer(turned(k[m]), v[m] * out_w), meta)

    for i, members in enumerate(rounds):
        for m in members:
            local_state(m)
        if i == 0:
            near_groups = 0
            for d in range(1, reach + 1):
                near_groups += lax.div(z + groups - d, groups) + lax.div(2 * groups - 1 - z - d, groups)
            pl.semaphore_wait(barrier, near_groups + (heads - 1) + (n_head - 1))
        post(0, members)
    local_state(pos)

    cell_gap = (
        lax.broadcasted_iota(jnp.int32, (HEAD_DIM, HEAD_DIM), 0)
        - lax.broadcasted_iota(jnp.int32, (HEAD_DIM, HEAD_DIM), 1)
    ).astype(F32)

    def weigh(h):
        rate = rates[h]
        near_w = jnp.where(cell_gap >= 0.0, jnp.exp(-rate * jnp.maximum(cell_gap, 0.0)), 0.0)
        far_w = jnp.exp(-rate * (cell_gap + float(HEAD_DIM)))
        step = jnp.exp(jnp.broadcast_to(-rate * float(HEAD_DIM), (1, HEAD_DIM)))
        factors = []
        for _ in range(1, length // HEAD_DIM):
            factors.append(far_w)
            far_w = far_w * step
        for j, end in column_groups(length):
            for r in range(j, length, HEAD_DIM):
                for c in range(j, end, HEAD_DIM):
                    cell = jnp.zeros((HEAD_DIM, HEAD_DIM), F32)
                    if r >= c:
                        value = near_w if r == c else factors[(r - c) // HEAD_DIM - 1]
                        same = seg_col[r : r + HEAD_DIM] == seg_row[:, c : c + HEAD_DIM]
                        cell = jnp.where(same, value, 0.0)
                    w[h, r : r + HEAD_DIM, c : c + HEAD_DIM] = cell

    def score(h):
        triangle(a_hi, a_lo, h, split(q[h]), split(k[h]), w)

    def mix(h):
        triangle(p_hi, p_lo, h, split(grad[h]), split(v[h]), w)

    own_step = jnp.exp(jnp.broadcast_to(-rates[pos] * float(length), (1, HEAD_DIM)))
    own_group = jnp.exp(jnp.broadcast_to(-rates[pos] * float(length * heads), (1, HEAD_DIM)))

    def on_group(t, d, c, action):
        there = z + d if t == 0 else z - d
        ok = there < groups if t == 0 else there >= 0

        @pl.when(ok)
        def _():
            action(remote(
                gsend.at[t, c], ginbox.at[t, d - 1, c], gr_s.at[t, d - 1, c], gr_r.at[t, d - 1, c],
                seq=there * heads + pos,
            ))

    def direction(t):
        order = list(range(heads))
        return (order, ROWS, ROWS + 1) if t == 0 else (order[::-1], ROWS + 1, ROWS)

    def gather_group(t, c):
        inbox[t, pos, c] = loc[t, pos, c]
        for p in range(heads):
            @pl.when(p != pos)
            def _(p=p):
                remote(
                    loc.at[t, p, c], inbox.at[t, p, c], st_s.at[t, p, c], st_r.at[t, p, c], seq=base + p
                ).wait_recv()
        order, near, far = direction(t)
        total = None
        for i, p in enumerate(order):
            state = inbox[t, p, c, :ROWS]
            if i > 0:
                before = order[i - 1]
                keep = inbox[t, before, c, near : near + 1] == inbox[t, p, c, far : far + 1]
                came = jnp.where(keep, total, 0.0)
                csend[t, p, c] = came
                through = inbox[t, p, c, near : near + 1] == inbox[t, p, c, far : far + 1]
                total = state + jnp.where(through, own_step, 0.0) * came
            else:
                total = state
        gsend[t, c, :ROWS] = total
        gsend[t, c, ROWS:] = jnp.broadcast_to(inbox[t, order[-1], c, near : near + 1], (8, HEAD_DIM))
        for d in range(1, reach + 1):
            on_group(t, d, c, lambda copy: copy.start())

    def carry_out(t, c):
        order, near, far = direction(t)
        for d in range(1, reach + 1):
            there = z - d if t == 0 else z + d
            ok = there >= 0 if t == 0 else there < groups

            @pl.when(ok)
            def _(d=d):
                remote(
                    gsend.at[t, c], ginbox.at[t, d - 1, c], gr_s.at[t, d - 1, c], gr_r.at[t, d - 1, c],
                    seq=lax.rem(me + heads, n_seq),
                ).wait_recv()

            @pl.when(jnp.logical_not(ok))
            def _(d=d):
                ginbox[t, d - 1, c] = jnp.full((PAD, HEAD_DIM), -1.0, F32)
        enter = jnp.zeros((ROWS, HEAD_DIM), F32)
        factor = jnp.ones((1, HEAD_DIM), F32)
        for d in range(1, reach + 1):
            keep = ginbox[t, d - 1, c, ROWS : ROWS + 1] == inbox[t, order[0], c, far : far + 1]
            enter = enter + jnp.where(keep, factor, 0.0) * ginbox[t, d - 1, c, :ROWS]
            factor = factor * own_group
        factor = jnp.ones((1, HEAD_DIM), F32)
        for i, p in enumerate(order):
            if i == 0:
                csend[t, p, c] = enter
            else:
                before = order[i - 1]
                through = (
                    (inbox[t, before, c, near : near + 1] == inbox[t, p, c, far : far + 1])
                    & (inbox[t, before, c, near : near + 1] == inbox[t, before, c, far : far + 1])
                )
                factor = factor * jnp.where(through, own_step, 0.0)
                csend[t, p, c] = csend[t, p, c] + factor * enter
        for m in peers:
            remote(
                csend.at[t, m, c], carry.at[t, pos, c], ca_s.at[t, m, c], ca_r.at[t, pos, c], seq=base + m
            ).start()
        carry[t, pos, c] = csend[t, pos, c]

    def wait_carry(t, m):
        for c in range(CHUNKS):
            remote(
                csend.at[t, m, c], carry.at[t, m, c], ca_s.at[t, m, c], ca_r.at[t, m, c], seq=base + m
            ).wait_recv()

    def carried(t, h):
        return split(carry[t, h].reshape(HEAD_DIM, HEAD_DIM))

    def weave(work, steps, lead):
        rest = max(len(work) - lead, 1)
        done = 0
        for i, piece in enumerate(work):
            piece()
            due = (i + 1 - lead) * len(steps) // rest if i + 1 > lead else 0
            while done < min(due, len(steps)):
                steps[done]()
                done += 1
        while done < len(steps):
            steps[done]()
            done += 1

    def turn(h):
        q_t[h] = turned(q[h])

    def intra(h):
        out[h] = by_rows(a_hi, a_lo, h, split(v[h]))

    def each(f):
        return [functools.partial(f, h) for h in range(heads)]

    def chunks(f, t):
        return [functools.partial(f, t, c) for c in range(CHUNKS)]

    for h in range(heads):
        weigh(h)
    for h in range(heads):
        load(2, h).wait()
    weave(each(score) + each(turn) + each(intra), chunks(gather_group, 0) + chunks(carry_out, 0), 1)
    for h in range(heads):
        load(3, h).wait()
    def shape_grad(h):
        grad[h] = g[h] * gain_ref[:, lanes_of(h)]

    for h in range(heads):
        shape_grad(h)
    squares = jnp.zeros((length, HEAD_DIM), F32)
    product = jnp.zeros((length, HEAD_DIM), F32)
    for m in [pos] + peers[::-1]:
        if m is not pos:
            wait_carry(0, m)
        o = out[m] + cols[0, m] * square_by_rows(split(q[m]), carried(0, m))
        out[m] = o
        squares = squares + o * o
        product = product + grad[m] * o
    sums = cat([
        jnp.sum(squares.T, axis=0, keepdims=True),
        jnp.sum(product.T, axis=0, keepdims=True),
        jnp.zeros((6, length), F32),
    ], 0)
    hsend[...] = sums
    for o in range(1, n_head):
        other = lax.rem(hx + o, n_head)
        remote(hsend, hinbox.at[hx], hd_s.at[o], hd_r.at[hx], head=other).start()
    hinbox[hx] = sums
    for o in range(1, n_head):
        other = lax.rem(hx + o, n_head)
        remote(hsend, hinbox.at[other], hd_s.at[o], hd_r.at[other], head=other).wait_recv()
    sums = hinbox[0]
    for i in range(1, n_head):
        sums = sums + hinbox[i]
    inv_row = lax.rsqrt(sums[0:1] / features + EPSILON)
    coef_row = inv_row * inv_row * inv_row * (sums[1:2] / features)
    inv = jnp.broadcast_to(inv_row, (HEAD_DIM, length)).T
    coef = jnp.broadcast_to(coef_row, (HEAD_DIM, length)).T

    def local_back(m):
        o = out[m]
        d_out = inv * grad[m] - coef * o
        grad[m] = d_out
        back_w = jnp.exp(-rates[m] * place) * head_first
        part = jnp.sum(g[m] * o * inv, axis=0, keepdims=True)
        put(1, m, outer(q_t[m], d_out * back_w), jnp.where(row_id == 2, part, meta))

    for members in rounds:
        for m in members:
            local_back(m)
        post(1, members)
    local_back(pos)

    def group_gain():
        part = inbox[1, 0, 0, ROWS:]
        for p in range(1, heads):
            part = part + inbox[1, p, 0, ROWS:]
        tsend[...] = part
        tinbox[pos] = part
        for m in peers:
            remote(tsend, tinbox.at[pos], nt_s.at[m], nt_r.at[pos], seq=base + m).start()

    def pass_gain(far, action):
        for t, source, there in ((0, z - far, z + 1), (1, z + far, z - 1)):
            ok = (source >= 0) & (there < groups) if t == 0 else (source < groups) & (there >= 0)

            @pl.when(ok)
            def _(t=t, source=source, there=there):
                action(remote(
                    ninbox.at[source], ninbox.at[source], ng_s.at[t, far], ng_r.at[source], seq=there * heads + pos
                ))

    def take_gain(far):
        for ok, source, there in ((z >= far, z - far, z - 1), (z + far < groups, z + far, z + 1)):
            @pl.when(ok)
            def _(source=source, there=there):
                remote(
                    ninbox.at[source], ninbox.at[source], ng_s.at[0, far], ng_r.at[source], seq=there * heads + pos
                ).wait_recv()

    def own_gain():
        for m in peers:
            remote(tsend, tinbox.at[m], nt_s.at[m], nt_r.at[m], seq=base + m).wait_recv()
        rows = [tinbox[h, 2:3] for h in range(heads)]
        rows += [jnp.zeros((1, HEAD_DIM), F32)] * (8 - heads)
        ninbox[z] = cat(rows, 0)
        pass_gain(0, lambda copy: copy.start())

    def move_gain(far):
        take_gain(far)
        pass_gain(far, lambda copy: copy.start())

    def for_queries(h):
        lanes = pl.ds(h * HEAD_DIM, HEAD_DIM)
        part = by_rows(p_hi, p_lo, h, split(k[h]))
        part = part + cols[0, h] * square_by_cols(split(grad[h]), carried(0, h))
        qg_ref[:, lanes] = part.astype(BF16)

    def for_keys(h):
        out[h] = under(q_t[h], p_hi, p_lo, h)

    def for_values(h):
        g[h] = under(turned(grad[h]), a_hi, a_lo, h)

    steps = chunks(gather_group, 1) + [group_gain] + chunks(carry_out, 1)
    steps += [own_gain] + [functools.partial(move_gain, far) for far in range(1, reach + 1)]
    weave(each(mix) + each(for_queries) + each(for_keys) + each(for_values), steps, heads)
    for m in [pos] + peers[::-1]:
        if m is not pos:
            wait_carry(1, m)
        state = carried(1, m)
        kg_ref[:, lanes_of(m)] = (out[m] + cols[1, m] * square_by_cols(split(v[m]), state)).astype(BF16)
        vg_ref[:, lanes_of(m)] = (g[m] + cols[1, m] * square_by_rows(split(k[m]), state)).astype(BF16)
    for far in range(reach + 1, groups):
        move_gain(far)
    part = ninbox[0]
    for i in range(1, groups):
        part = part + ninbox[i]
    for h in range(heads):
        gain_out[:, h * HEAD_DIM : (h + 1) * HEAD_DIM] = part[h : h + 1]

    for t in range(2):
        for c in range(CHUNKS):
            for m in peers:
                remote(
                    loc.at[t, m, c], inbox.at[t, pos, c], st_s.at[t, m, c], st_r.at[t, pos, c], seq=base + m
                ).wait_send()
                remote(
                    csend.at[t, m, c], carry.at[t, pos, c], ca_s.at[t, m, c], ca_r.at[t, pos, c], seq=base + m
                ).wait_send()
            for d in range(1, reach + 1):
                on_group(t, d, c, lambda copy: copy.wait_send())
    for o in range(1, n_head):
        remote(hsend, hinbox.at[hx], hd_s.at[o], hd_r.at[hx], head=lax.rem(hx + o, n_head)).wait_send()
    for far in range(groups):
        pass_gain(far, lambda copy: copy.wait_send())
    for m in peers:
        remote(tsend, tinbox.at[pos], nt_s.at[m], nt_r.at[pos], seq=base + m).wait_send()


def store(*refs):
    sem = refs[-1]
    copies = [pltpu.make_async_copy(refs[i], refs[4 + i], sem.at[i]) for i in range(4)]
    for copy in copies:
        copy.start()
    for copy in copies:
        copy.wait()


def body(n_seq, n_head, queries, key_vectors, value_vectors, out_grad, norm_gain, decay_rates, segment_ids):
    length, width = queries.shape
    heads = width // HEAD_DIM
    groups = n_seq // heads
    longest = (length * n_seq) // 3
    blocks = -(-(longest - 1) // length)
    reach = min(-(-blocks // heads), groups - 1)
    shape = (heads, length, n_seq, n_head, groups, reach)
    any_spec = pl.BlockSpec(memory_space=pl.ANY)
    vmem = pl.BlockSpec(memory_space=pltpu.VMEM)
    tok = (heads, length, HEAD_DIM)
    sq = (heads, length, length)
    dma = pltpu.SemaphoreType.DMA
    outs = pl.pallas_call(
        functools.partial(kernel, shape),
        out_shape=(
            jax.ShapeDtypeStruct((length, width), BF16),
            jax.ShapeDtypeStruct((length, width), BF16),
            jax.ShapeDtypeStruct((length, width), BF16),
            jax.ShapeDtypeStruct((1, width), F32),
        ),
        in_specs=[any_spec] * 4 + [vmem, pl.BlockSpec(memory_space=pltpu.SMEM), vmem],
        out_specs=(vmem,) * 4,
        scratch_shapes=[
            pltpu.VMEM(tok, F32), pltpu.VMEM(tok, F32), pltpu.VMEM(tok, F32), pltpu.VMEM(tok, F32),
            pltpu.VMEM(sq, F32),
            pltpu.VMEM(sq, BF16), pltpu.VMEM(sq, BF16), pltpu.VMEM(sq, BF16), pltpu.VMEM(sq, BF16),
            pltpu.VMEM(tok, F32), pltpu.VMEM(tok, F32),
            pltpu.VMEM((2,) + tok, F32),
            pltpu.VMEM((heads, 2 * HEAD_DIM, length), BF16),
            pltpu.VMEM((2, heads, CHUNKS, PAD, HEAD_DIM), F32),
            pltpu.VMEM((2, heads, CHUNKS, PAD, HEAD_DIM), F32),
            pltpu.VMEM((2, CHUNKS, PAD, HEAD_DIM), F32),
            pltpu.VMEM((2, reach, CHUNKS, PAD, HEAD_DIM), F32),
            pltpu.VMEM((2, heads, CHUNKS, ROWS, HEAD_DIM), F32),
            pltpu.VMEM((2, heads, CHUNKS, ROWS, HEAD_DIM), F32),
            pltpu.VMEM((8, length), F32),
            pltpu.VMEM((n_head, 8, length), F32),
            pltpu.VMEM((groups, 8, HEAD_DIM), F32),
            pltpu.VMEM((8, HEAD_DIM), F32),
            pltpu.VMEM((heads, 8, HEAD_DIM), F32),
            dma((4, heads)),
            dma((2, heads, CHUNKS)), dma((2, heads, CHUNKS)),
            dma((2, reach, CHUNKS)), dma((2, reach, CHUNKS)),
            dma((2, heads, CHUNKS)), dma((2, heads, CHUNKS)),
            dma((n_head,)), dma((n_head,)),
            dma((2, groups)), dma((groups,)),
            dma((heads,)), dma((heads,)),
        ],
        compiler_params=pltpu.CompilerParams(
            collective_id=0, has_side_effects=True, vmem_limit_bytes=VMEM_BYTES
        ),
        name="decayed_attention_grad",
    )(
        queries, key_vectors, value_vectors, out_grad,
        norm_gain.reshape(1, width), decay_rates, segment_ids,
    )
    outs = pl.pallas_call(
        store,
        out_shape=tuple(jax.ShapeDtypeStruct(x.shape, x.dtype) for x in outs),
        in_specs=[vmem] * 4,
        out_specs=(any_spec,) * 4,
        scratch_shapes=[dma((4,))],
        compiler_params=pltpu.CompilerParams(vmem_limit_bytes=VMEM_BYTES),
        name="store_results",
    )(*outs)
    return outs[0], outs[1], outs[2], outs[3].reshape(width)


def solution(mesh):
    return jax.shard_map(
        functools.partial(body, mesh.shape["seq"], mesh.shape["head"]),
        mesh=mesh,
        in_specs=(
            P("seq", "head"),
            P("seq", "head"),
            P("seq", "head"),
            P("seq", "head"),
            P("head"),
            P("head"),
            P("seq"),
        ),
        out_specs=(P("seq", "head"), P("seq", "head"), P("seq", "head"), P("head")),
        check_vma=False,
    )
```

```python
import functools

import jax
import jax.numpy as jnp
from jax import lax
from jax.experimental import pallas as pl
from jax.experimental.pallas import tpu as pltpu
from jax.sharding import PartitionSpec as P

HEAD_DIM = 128
CHUNKS = 2
ROWS = HEAD_DIM // CHUNKS
PAD = ROWS + 8
CORES = 2
GROUP = 256
VMEM_BYTES = 63 * 1024 * 1024
EPSILON = 1e-06
F32 = jnp.float32
BF16 = jnp.bfloat16


def split(x):
    hi = x.astype(BF16)
    return hi, (x - hi.astype(F32)).astype(BF16)


def dot(a, b, ca, cb):
    return lax.dot_general(a, b, (((ca,), (cb,)), ((), ())), preferred_element_type=F32)


def cat(parts, axis=1):
    return jnp.concatenate(parts, axis=axis)


def rows_by_rows(a, b):
    return dot(cat([a[0], a[1], a[0]]), cat([b[0], b[0], b[1]]), 1, 1)


def fold(both):
    return both[:, :HEAD_DIM] + both[:, HEAD_DIM:]


def square_by_rows(a, b):
    half = cat([b[0], b[1]])
    return fold(dot(cat(list(a)), cat([half, half], 0), 1, 0))


def square_by_cols(a, b):
    half = cat([b[0], b[1]], 0)
    return fold(dot(cat(list(a)), cat([half, half]), 1, 1))


def turned(x):
    return cat(list(split(x.T)), 0)


def outer(a_t, b):
    both = fold(dot(a_t, cat(list(split(b))), 1, 0))
    return both[:HEAD_DIM] + both[HEAD_DIM:]


def column_groups(length):
    return [(j, min(j + GROUP, length)) for j in range(0, length, GROUP)]


def under(a_t, hi, lo, h):
    length = hi.shape[1]
    parts = []
    for j, end in column_groups(length):
        both = dot(a_t[:, j:], hi[h, j:, j:end], 1, 0)
        part = both[:HEAD_DIM] + both[HEAD_DIM:] + dot(a_t[:HEAD_DIM, j:], lo[h, j:, j:end], 1, 0)
        parts.append(part.T)
    return cat(parts, 0)


def by_rows(hi, lo, h, b):
    length = hi.shape[1]
    both = cat(list(b))
    total = None
    for j, end in column_groups(length):
        part = fold(dot(hi[h, j:, j:end], both[j:end], 1, 0)) + dot(lo[h, j:, j:end], b[0][j:end], 1, 0)
        total = part if total is None else cat([total[:j], total[j:] + part], 0)
    return total


def triangle(hi, lo, h, a, b, w):
    length = hi.shape[1]
    for j, end in column_groups(length):
        part = rows_by_rows([x[j:] for x in a], [x[j:end] for x in b]) * w[h, j:, j:end]
        hi[h, j:, j:end], lo[h, j:, j:end] = split(part)


def kernel(
    shape, q_hbm, k_hbm, v_hbm, g_hbm, gain_ref, rates, seg_ref,
    qg_hbm, kg_hbm, vg_hbm, gain_out, qg_ref, kg_ref, vg_ref,
    q, k, v, g, w, a_hi, a_lo, p_hi, p_lo, out, grad, cols, q_t,
    loc, inbox, gsend, ginbox, csend, carry,
    hsend, hinbox, nsend, ninbox, tsend, tinbox,
    in_sem, out_sem, st_s, st_r, gr_s, gr_r, ca_s, ca_r, hd_s, hd_r, ng_s, ng_r, nt_s, nt_r,
):
    heads, length, n_seq, n_head, groups, reach = shape
    me = lax.axis_index("seq")
    hx = lax.axis_index("head")
    pos = lax.rem(me, heads)
    z = lax.div(me, heads)
    base = z * heads
    features = float(heads * HEAD_DIM * n_head)

    def lanes_of(h):
        return pl.ds(pl.multiple_of(h * HEAD_DIM, HEAD_DIM), HEAD_DIM)

    def load(i, h):
        src, dst = ((k_hbm, k), (v_hbm, v), (q_hbm, q), (g_hbm, g))[i]
        return pltpu.make_async_copy(
            src.at[:, lanes_of(h)], dst.at[h], in_sem.at[i, h]
        )

    side = lax.div(pos, CORES)
    sides = heads // CORES

    def others(o):
        there = lax.rem(side + o, sides) * CORES
        return [there + i for i in range(CORES)]

    mates = [side * CORES + lax.rem(pos - side * CORES + i, CORES) for i in range(1, CORES)]
    rounds = [others(o) for o in range(1, sides)] + [mates]
    peers = [m for members in rounds for m in members]

    for m in peers + [pos]:
        load(0, m).start()
        load(1, m).start()
    for i in (2, 3):
        for m in range(heads):
            load(i, m).start()

    def keep(i, h):
        src, dst = ((qg_ref, qg_hbm), (kg_ref, kg_hbm), (vg_ref, vg_hbm))[i]
        return pltpu.make_async_copy(src.at[:, lanes_of(h)], dst.at[:, lanes_of(h)], out_sem.at[i, h])

    def remote(src, dst, ss, rs, **where):
        return pltpu.make_async_remote_copy(
            src_ref=src, dst_ref=dst, send_sem=ss, recv_sem=rs,
            device_id=where, device_id_type=pl.DeviceIdType.MESH,
        )

    barrier = pltpu.get_barrier_semaphore()

    def greet(**where):
        pl.semaphore_signal(barrier, inc=1, device_id=where, device_id_type=pl.DeviceIdType.MESH)

    for o in range(1, heads):
        greet(seq=base + lax.rem(pos + o, heads))
    for o in range(1, groups):
        greet(seq=lax.rem(z + o, groups) * heads + pos)
    for o in range(1, n_head):
        greet(head=lax.rem(hx + o, n_head))

    seg_row = seg_ref[...].reshape(1, length).astype(F32)
    first = seg_row[0:1, 0:1]
    last = seg_row[0:1, length - 1 : length]
    seg_col = jnp.broadcast_to(seg_row, (HEAD_DIM, length)).T
    place = lax.broadcasted_iota(jnp.int32, (length, HEAD_DIM), 0).astype(F32)
    head_first = jnp.where(seg_col == first, 1.0, 0.0)
    tail_last = jnp.where(seg_col == last, 1.0, 0.0)
    for h in range(heads):
        rate = rates[h]
        cols[0, h] = jnp.exp(-rate * (place + 1.0)) * head_first
        cols[1, h] = jnp.exp(-rate * (length - place)) * tail_last

    def post(t, members):
        for c in range(CHUNKS):
            for m in members:
                remote(
                    loc.at[t, m, c], inbox.at[t, pos, c], st_s.at[t, m, c], st_r.at[t, pos, c], seq=base + m
                ).start()

    def put(t, m, state, tail):
        for c in range(CHUNKS):
            loc[t, m, c, :ROWS] = state[c * ROWS : (c + 1) * ROWS]
            loc[t, m, c, ROWS:] = tail

    row_id = lax.broadcasted_iota(jnp.int32, (8, HEAD_DIM), 0)
    meta = jnp.where(row_id == 0, last, jnp.where(row_id == 1, first, 0.0))

    def local_state(m):
        load(0, m).wait()
        load(1, m).wait()
        out_w = jnp.exp(-rates[m] * (length - 1.0 - place)) * tail_last
        put(0, m, outer(turned(k[m]), v[m] * out_w), meta)

    for i, members in enumerate(rounds):
        for m in members:
            local_state(m)
        if i == 0:
            pl.semaphore_wait(barrier, (heads - 1) + (groups - 1) + (n_head - 1))
        post(0, members)
    local_state(pos)

    cell_gap = (
        lax.broadcasted_iota(jnp.int32, (HEAD_DIM, HEAD_DIM), 0)
        - lax.broadcasted_iota(jnp.int32, (HEAD_DIM, HEAD_DIM), 1)
    ).astype(F32)

    def weigh(h):
        rate = rates[h]
        near_w = jnp.where(cell_gap >= 0.0, jnp.exp(-rate * jnp.maximum(cell_gap, 0.0)), 0.0)
        far_w = jnp.exp(-rate * (cell_gap + float(HEAD_DIM)))
        step = jnp.exp(jnp.broadcast_to(-rate * float(HEAD_DIM), (1, HEAD_DIM)))
        factors = []
        for _ in range(1, length // HEAD_DIM):
            factors.append(far_w)
            far_w = far_w * step
        for j, end in column_groups(length):
            for r in range(j, length, HEAD_DIM):
                for c in range(j, end, HEAD_DIM):
                    cell = jnp.zeros((HEAD_DIM, HEAD_DIM), F32)
                    if r >= c:
                        value = near_w if r == c else factors[(r - c) // HEAD_DIM - 1]
                        same = seg_col[r : r + HEAD_DIM] == seg_row[:, c : c + HEAD_DIM]
                        cell = jnp.where(same, value, 0.0)
                    w[h, r : r + HEAD_DIM, c : c + HEAD_DIM] = cell

    def score(h):
        triangle(a_hi, a_lo, h, split(q[h]), split(k[h]), w)

    def mix(h):
        triangle(p_hi, p_lo, h, split(grad[h]), split(v[h]), w)

    own_step = jnp.exp(jnp.broadcast_to(-rates[pos] * float(length), (1, HEAD_DIM)))
    own_group = jnp.exp(jnp.broadcast_to(-rates[pos] * float(length * heads), (1, HEAD_DIM)))

    def on_group(t, d, c, action):
        there = z + d if t == 0 else z - d
        ok = there < groups if t == 0 else there >= 0

        @pl.when(ok)
        def _():
            action(remote(
                gsend.at[t, c], ginbox.at[t, d - 1, c], gr_s.at[t, d - 1, c], gr_r.at[t, d - 1, c],
                seq=there * heads + pos,
            ))

    def direction(t):
        order = list(range(heads))
        return (order, ROWS, ROWS + 1) if t == 0 else (order[::-1], ROWS + 1, ROWS)

    def gather_group(t, c):
        inbox[t, pos, c] = loc[t, pos, c]
        for p in range(heads):
            @pl.when(p != pos)
            def _(p=p):
                remote(
                    loc.at[t, p, c], inbox.at[t, p, c], st_s.at[t, p, c], st_r.at[t, p, c], seq=base + p
                ).wait_recv()
        order, near, far = direction(t)
        total = None
        for i, p in enumerate(order):
            state = inbox[t, p, c, :ROWS]
            if i > 0:
                before = order[i - 1]
                keep = inbox[t, before, c, near : near + 1] == inbox[t, p, c, far : far + 1]
                came = jnp.where(keep, total, 0.0)
                csend[t, p, c] = came
                through = inbox[t, p, c, near : near + 1] == inbox[t, p, c, far : far + 1]
                total = state + jnp.where(through, own_step, 0.0) * came
            else:
                total = state
        gsend[t, c, :ROWS] = total
        gsend[t, c, ROWS:] = jnp.broadcast_to(inbox[t, order[-1], c, near : near + 1], (8, HEAD_DIM))
        for d in range(1, reach + 1):
            on_group(t, d, c, lambda copy: copy.start())

    def carry_out(t, c):
        order, near, far = direction(t)
        for d in range(1, reach + 1):
            there = z - d if t == 0 else z + d
            ok = there >= 0 if t == 0 else there < groups

            @pl.when(ok)
            def _(d=d):
                remote(
                    gsend.at[t, c], ginbox.at[t, d - 1, c], gr_s.at[t, d - 1, c], gr_r.at[t, d - 1, c],
                    seq=lax.rem(me + heads, n_seq),
                ).wait_recv()

            @pl.when(jnp.logical_not(ok))
            def _(d=d):
                ginbox[t, d - 1, c] = jnp.full((PAD, HEAD_DIM), -1.0, F32)
        enter = jnp.zeros((ROWS, HEAD_DIM), F32)
        factor = jnp.ones((1, HEAD_DIM), F32)
        for d in range(1, reach + 1):
            keep = ginbox[t, d - 1, c, ROWS : ROWS + 1] == inbox[t, order[0], c, far : far + 1]
            enter = enter + jnp.where(keep, factor, 0.0) * ginbox[t, d - 1, c, :ROWS]
            factor = factor * own_group
        factor = jnp.ones((1, HEAD_DIM), F32)
        for i, p in enumerate(order):
            if i == 0:
                csend[t, p, c] = enter
            else:
                before = order[i - 1]
                through = (
                    (inbox[t, before, c, near : near + 1] == inbox[t, p, c, far : far + 1])
                    & (inbox[t, before, c, near : near + 1] == inbox[t, before, c, far : far + 1])
                )
                factor = factor * jnp.where(through, own_step, 0.0)
                csend[t, p, c] = csend[t, p, c] + factor * enter
        for m in peers:
            remote(
                csend.at[t, m, c], carry.at[t, pos, c], ca_s.at[t, m, c], ca_r.at[t, pos, c], seq=base + m
            ).start()
        carry[t, pos, c] = csend[t, pos, c]

    def wait_carry(t, m):
        for c in range(CHUNKS):
            remote(
                csend.at[t, m, c], carry.at[t, m, c], ca_s.at[t, m, c], ca_r.at[t, m, c], seq=base + m
            ).wait_recv()

    def carried(t, h):
        return split(carry[t, h].reshape(HEAD_DIM, HEAD_DIM))

    def weave(work, steps, lead):
        rest = max(len(work) - lead, 1)
        done = 0
        for i, piece in enumerate(work):
            piece()
            due = (i + 1 - lead) * len(steps) // rest if i + 1 > lead else 0
            while done < min(due, len(steps)):
                steps[done]()
                done += 1
        while done < len(steps):
            steps[done]()
            done += 1

    def turn(h):
        q_t[h] = turned(q[h])

    def intra(h):
        out[h] = by_rows(a_hi, a_lo, h, split(v[h]))

    def each(f):
        return [functools.partial(f, h) for h in range(heads)]

    def chunks(f, t):
        return [functools.partial(f, t, c) for c in range(CHUNKS)]

    for h in range(heads):
        weigh(h)
    for h in range(heads):
        load(2, h).wait()
    weave(each(score) + each(turn) + each(intra), chunks(gather_group, 0) + chunks(carry_out, 0), 1)
    for h in range(heads):
        load(3, h).wait()
    def shape_grad(h):
        grad[h] = g[h] * gain_ref[:, lanes_of(h)]

    for h in range(heads):
        shape_grad(h)
    squares = jnp.zeros((length, HEAD_DIM), F32)
    product = jnp.zeros((length, HEAD_DIM), F32)
    for m in [pos] + peers[::-1]:
        if m is not pos:
            wait_carry(0, m)
        o = out[m] + cols[0, m] * square_by_rows(split(q[m]), carried(0, m))
        out[m] = o
        squares = squares + o * o
        product = product + grad[m] * o
    sums = cat([
        jnp.sum(squares.T, axis=0, keepdims=True),
        jnp.sum(product.T, axis=0, keepdims=True),
        jnp.zeros((6, length), F32),
    ], 0)
    hsend[...] = sums
    for o in range(1, n_head):
        other = lax.rem(hx + o, n_head)
        remote(hsend, hinbox.at[hx], hd_s.at[o], hd_r.at[hx], head=other).start()
    hinbox[hx] = sums
    for o in range(1, n_head):
        other = lax.rem(hx + o, n_head)
        remote(hsend, hinbox.at[other], hd_s.at[o], hd_r.at[other], head=other).wait_recv()
    sums = hinbox[0]
    for i in range(1, n_head):
        sums = sums + hinbox[i]
    inv_row = lax.rsqrt(sums[0:1] / features + EPSILON)
    coef_row = inv_row * inv_row * inv_row * (sums[1:2] / features)
    inv = jnp.broadcast_to(inv_row, (HEAD_DIM, length)).T
    coef = jnp.broadcast_to(coef_row, (HEAD_DIM, length)).T

    def local_back(m):
        o = out[m]
        d_out = inv * grad[m] - coef * o
        grad[m] = d_out
        back_w = jnp.exp(-rates[m] * place) * head_first
        part = jnp.sum(g[m] * o * inv, axis=0, keepdims=True)
        put(1, m, outer(q_t[m], d_out * back_w), jnp.where(row_id == 2, part, meta))

    for members in rounds:
        for m in members:
            local_back(m)
        post(1, members)
    local_back(pos)

    def group_gain():
        part = inbox[1, 0, 0, ROWS:]
        for p in range(1, heads):
            part = part + inbox[1, p, 0, ROWS:]
        nsend[...] = part
        ninbox[z] = part
        for o in range(1, groups):
            other = lax.rem(z + o, groups)
            remote(nsend, ninbox.at[z], ng_s.at[o], ng_r.at[z], seq=other * heads + pos).start()

    def whole_gain():
        for o in range(1, groups):
            other = lax.rem(z + o, groups)
            remote(nsend, ninbox.at[other], ng_s.at[o], ng_r.at[other], seq=other * heads + pos).wait_recv()
        part = ninbox[0]
        for i in range(1, groups):
            part = part + ninbox[i]
        tsend[...] = part
        tinbox[pos] = part
        for p in range(heads):
            @pl.when(p != pos)
            def _(p=p):
                remote(tsend, tinbox.at[pos], nt_s.at[p], nt_r.at[pos], seq=base + p).start()

    def for_queries(h):
        lanes = pl.ds(h * HEAD_DIM, HEAD_DIM)
        part = by_rows(p_hi, p_lo, h, split(k[h]))
        part = part + cols[0, h] * square_by_cols(split(grad[h]), carried(0, h))
        qg_ref[:, lanes] = part.astype(BF16)
        keep(0, h).start()

    def for_keys(h):
        out[h] = under(q_t[h], p_hi, p_lo, h)

    def for_values(h):
        g[h] = under(turned(grad[h]), a_hi, a_lo, h)

    steps = chunks(gather_group, 1) + [group_gain] + chunks(carry_out, 1) + [whole_gain]
    weave(each(mix) + each(for_queries) + each(for_keys) + each(for_values), steps, heads)
    for m in [pos] + peers[::-1]:
        if m is not pos:
            wait_carry(1, m)
        state = carried(1, m)
        kg_ref[:, lanes_of(m)] = (out[m] + cols[1, m] * square_by_cols(split(v[m]), state)).astype(BF16)
        keep(1, m).start()
        vg_ref[:, lanes_of(m)] = (g[m] + cols[1, m] * square_by_rows(split(k[m]), state)).astype(BF16)
        keep(2, m).start()
    for p in range(heads):
        @pl.when(p != pos)
        def _(p=p):
            remote(tsend, tinbox.at[p], nt_s.at[p], nt_r.at[p], seq=base + p).wait_recv()
    for h in range(heads):
        gain_out[:, h * HEAD_DIM : (h + 1) * HEAD_DIM] = tinbox[h, 2:3]

    for i in range(3):
        for h in range(heads):
            keep(i, h).wait()
    for t in range(2):
        for c in range(CHUNKS):
            for m in peers:
                remote(
                    loc.at[t, m, c], inbox.at[t, pos, c], st_s.at[t, m, c], st_r.at[t, pos, c], seq=base + m
                ).wait_send()
                remote(
                    csend.at[t, m, c], carry.at[t, pos, c], ca_s.at[t, m, c], ca_r.at[t, pos, c], seq=base + m
                ).wait_send()
            for d in range(1, reach + 1):
                on_group(t, d, c, lambda copy: copy.wait_send())
    for o in range(1, n_head):
        remote(hsend, hinbox.at[hx], hd_s.at[o], hd_r.at[hx], head=lax.rem(hx + o, n_head)).wait_send()
    for o in range(1, groups):
        other = lax.rem(z + o, groups)
        remote(nsend, ninbox.at[z], ng_s.at[o], ng_r.at[z], seq=other * heads + pos).wait_send()
    for p in range(heads):
        @pl.when(p != pos)
        def _(p=p):
            remote(tsend, tinbox.at[pos], nt_s.at[p], nt_r.at[pos], seq=base + p).wait_send()


def store(*refs):
    ins, outs, held, sem = refs[:4], refs[4:8], refs[8:12], refs[12]
    here = [pltpu.make_async_copy(ins[i], held[i], sem.at[0, i]) for i in range(4)]
    away = [pltpu.make_async_copy(held[i], outs[i], sem.at[1, i]) for i in range(4)]
    for copy in here:
        copy.start()
    for first, second in zip(here, away):
        first.wait()
        second.start()
    for copy in away:
        copy.wait()


def body(n_seq, n_head, queries, key_vectors, value_vectors, out_grad, norm_gain, decay_rates, segment_ids):
    length, width = queries.shape
    heads = width // HEAD_DIM
    groups = n_seq // heads
    longest = (length * n_seq) // 3
    blocks = -(-(longest - 1) // length)
    reach = min(-(-blocks // heads), groups - 1)
    shape = (heads, length, n_seq, n_head, groups, reach)
    any_spec = pl.BlockSpec(memory_space=pl.ANY)
    vmem = pl.BlockSpec(memory_space=pltpu.VMEM)
    tok = (heads, length, HEAD_DIM)
    sq = (heads, length, length)
    dma = pltpu.SemaphoreType.DMA
    outs = pl.pallas_call(
        functools.partial(kernel, shape),
        out_shape=(
            jax.ShapeDtypeStruct((length, width), BF16),
            jax.ShapeDtypeStruct((length, width), BF16),
            jax.ShapeDtypeStruct((length, width), BF16),
            jax.ShapeDtypeStruct((1, width), F32),
        ),
        in_specs=[any_spec] * 4 + [vmem, pl.BlockSpec(memory_space=pltpu.SMEM), vmem],
        out_specs=(any_spec,) * 3 + (vmem,),
        scratch_shapes=[
            pltpu.VMEM((length, width), BF16), pltpu.VMEM((length, width), BF16), pltpu.VMEM((length, width), BF16),
            pltpu.VMEM(tok, F32), pltpu.VMEM(tok, F32), pltpu.VMEM(tok, F32), pltpu.VMEM(tok, F32),
            pltpu.VMEM(sq, F32),
            pltpu.VMEM(sq, BF16), pltpu.VMEM(sq, BF16), pltpu.VMEM(sq, BF16), pltpu.VMEM(sq, BF16),
            pltpu.VMEM(tok, F32), pltpu.VMEM(tok, F32),
            pltpu.VMEM((2,) + tok, F32),
            pltpu.VMEM((heads, 2 * HEAD_DIM, length), BF16),
            pltpu.VMEM((2, heads, CHUNKS, PAD, HEAD_DIM), F32),
            pltpu.VMEM((2, heads, CHUNKS, PAD, HEAD_DIM), F32),
            pltpu.VMEM((2, CHUNKS, PAD, HEAD_DIM), F32),
            pltpu.VMEM((2, reach, CHUNKS, PAD, HEAD_DIM), F32),
            pltpu.VMEM((2, heads, CHUNKS, ROWS, HEAD_DIM), F32),
            pltpu.VMEM((2, heads, CHUNKS, ROWS, HEAD_DIM), F32),
            pltpu.VMEM((8, length), F32),
            pltpu.VMEM((n_head, 8, length), F32),
            pltpu.VMEM((8, HEAD_DIM), F32),
            pltpu.VMEM((groups, 8, HEAD_DIM), F32),
            pltpu.VMEM((8, HEAD_DIM), F32),
            pltpu.VMEM((heads, 8, HEAD_DIM), F32),
            dma((4, heads)), dma((3, heads)),
            dma((2, heads, CHUNKS)), dma((2, heads, CHUNKS)),
            dma((2, reach, CHUNKS)), dma((2, reach, CHUNKS)),
            dma((2, heads, CHUNKS)), dma((2, heads, CHUNKS)),
            dma((n_head,)), dma((n_head,)),
            dma((groups,)), dma((groups,)),
            dma((heads,)), dma((heads,)),
        ],
        compiler_params=pltpu.CompilerParams(
            collective_id=0, has_side_effects=True, vmem_limit_bytes=VMEM_BYTES
        ),
        name="decayed_attention_grad",
    )(
        queries, key_vectors, value_vectors, out_grad,
        norm_gain.reshape(1, width), decay_rates, segment_ids,
    )
    outs = pl.pallas_call(
        store,
        out_shape=tuple(jax.ShapeDtypeStruct(x.shape, x.dtype) for x in outs),
        in_specs=[any_spec] * 4,
        out_specs=(any_spec,) * 4,
        scratch_shapes=[pltpu.VMEM(x.shape, x.dtype) for x in outs] + [dma((2, 4))],
        compiler_params=pltpu.CompilerParams(vmem_limit_bytes=VMEM_BYTES),
        name="store_results",
    )(*outs)
    return outs[0], outs[1], outs[2], outs[3].reshape(width)


def solution(mesh):
    return jax.shard_map(
        functools.partial(body, mesh.shape["seq"], mesh.shape["head"]),
        mesh=mesh,
        in_specs=(
            P("seq", "head"),
            P("seq", "head"),
            P("seq", "head"),
            P("seq", "head"),
            P("head"),
            P("head"),
            P("seq"),
        ),
        out_specs=(P("seq", "head"), P("seq", "head"), P("seq", "head"), P("head")),
        check_vma=False,
    )
```
